32 devices in a mesh: groups: 2 (over y), tile: 4 (over z), depth: 2 (over x), chan: 2 (over core).
Axes of the slice: x: 2, y: 2, z: 4, core: 2. Of those that a mesh axis runs over, the one named last changes fastest.
Arguments:
- log_features: bfloat16 [16, 64, 128, 128], P(('groups', 'tile', 'depth'), None, 'chan'), parts along dimension 0, may hold values from -3 to 3
- send_slot: int32 [16, 8, 16], P(('groups', 'tile', 'depth')), parts along dimension 0, may hold values from -1 to 63, as said below
- merge_slot: int32 [16, 8, 16], P(('groups', 'tile', 'depth')), parts along dimension 0, may hold values from -1 to 3, as said below
- halo_list: int32 [16, 4, 2], P(('groups', 'tile', 'depth')), parts along dimension 0, may hold values from 0 to 3, as said below
- in_rows: int32 [16, 27, 128], P(('groups', 'tile', 'depth')), parts along dimension 0, may hold values from 0 to 1535, as said below
- out_rows: int32 [16, 27, 128], P(('groups', 'tile', 'depth')), parts along dimension 0, may hold values from 0 to 511, as said below
- pair_count: int32 [16, 27], P(('groups', 'tile', 'depth')), parts along dimension 0, may hold values from 17 to 128
- weight: bfloat16 [27, 128, 128], replicated, may hold values from -0.1875 to 0.1875
- cotangent: bfloat16 [16, 4, 128, 128], P(('groups', 'tile', 'depth'), None, 'chan'), parts along dimension 0, may hold values from -6 to 6
Outputs:
- activations: bfloat16 [16, 4, 128, 128], P(('groups', 'tile', 'depth'), None, 'chan'), parts along dimension 0
- grad_log: bfloat16 [16, 64, 128, 128], P(('groups', 'tile', 'depth'), None, 'chan'), parts along dimension 0
- grad_weight: float32 [54, 128, 128], P('groups', 'chan'), parts along dimension 0
The draws below stay inside these ranges and needn't reach their ends.
There are 2 independent parts, one for each index of `groups`. The reference program is written for one: setup_inputs(seed, part) draws one part's arguments, and reference() takes and returns one part's arrays. A program takes and returns all parts, laid end to end along the dimension named above; an argument that names none is the same for every part. Nothing has to cross between parts.
Inputs may be any that keep to these rules, and one draw needn't show every extreme that they name: send_slot[s, p, c] is the log block of shard s in slot c towards tile p, or -1 for an empty slot; every log block of a shard occupies exactly one slot; one tile, the same for every shard, receives a full 16 slots from every shard and the remaining blocks go to the other tiles. merge_slot[p, s, c] is -1 exactly where send_slot[s, p, c] is -1. The 2 entries of halo_list[t, d] are distinct; d = 0, 1, 2, 3 is the neighbour t - 2, t + 2, t - 1, t + 1. `in_rows`: entries of one tile and offset are distinct; entries at positions from pair_count on are padding. `out_rows`: entries of one tile and offset are distinct; entries at positions from pair_count on are padding.
All inputs are finite; a program needn't handle non-finite values.
Results may differ from the reference program's by a relative error of at most 0.0058.
Values may be sent and summed in bfloat16 or wider, within the bound.
No kernel may reach another device: no remote copies, remote signals or barrier semaphores. Data moves between devices by JAX's collectives and lax.ppermute only.
A program may use at most 64 MiB of HBM per device.

```python
import jax
import jax.numpy as jnp
from jax import lax

CHANNELS = 128
BLOCK = 128
OFFSETS = 27
RIM_BLOCKS = 2
TILE_BLOCKS = 4
LOG_BLOCKS = 64
PAIRS = 128
TILE_ROWS = 4
DEPTHS = 2
TILES = 8
CAPACITY = 16
EXT_BLOCKS = 12


def route_tables(key):
    hot_tile = jax.random.randint(jax.random.fold_in(key, 101), (), 0, TILES)
    other_slots = (TILES - 1) * CAPACITY
    source_keys = jax.random.split(jax.random.fold_in(key, 102), TILES)

    def one_source(source_key):
        order_key, block_key = jax.random.split(source_key)
        chosen = jax.random.permutation(order_key, other_slots)[:LOG_BLOCKS - CAPACITY]
        shuffled = jax.random.permutation(block_key, LOG_BLOCKS).astype(jnp.int32)
        other_peer = chosen // CAPACITY
        peer_index = jnp.where(other_peer >= hot_tile, other_peer + 1, other_peer)
        flat_slots = jnp.concatenate([hot_tile * CAPACITY + jnp.arange(CAPACITY, dtype=jnp.int32), (peer_index * CAPACITY + chosen % CAPACITY).astype(jnp.int32)])
        table = jnp.full((TILES * CAPACITY,), -1, jnp.int32).at[flat_slots].set(shuffled)
        return table.reshape(TILES, CAPACITY)
    send_table = jax.vmap(one_source)(source_keys)
    targets = jax.random.randint(jax.random.fold_in(key, 103), (TILES, TILES, CAPACITY), 0, TILE_BLOCKS)
    merge_table = jnp.where(jnp.transpose(send_table, (1, 0, 2)) >= 0, targets, -1)
    return (send_table, merge_table.astype(jnp.int32))


def draw_send_slot(key, part):
    return route_tables(key)[0]


def draw_merge_slot(key, part):
    return route_tables(key)[1]


def draw_halo_list(key, part):
    key = jax.random.fold_in(key, 7)
    keys = jax.random.split(key, TILES * 4)
    picks = jax.vmap(lambda one_key: jax.random.permutation(one_key, TILE_BLOCKS)[:RIM_BLOCKS])(keys)
    return picks.reshape(TILES, 4, RIM_BLOCKS).astype(jnp.int32)


def draw_in_rows(key, part):
    key = jax.random.fold_in(key, 8)
    keys = jax.random.split(key, TILES * OFFSETS)
    picks = jax.vmap(lambda one_key: jax.random.permutation(one_key, EXT_BLOCKS * BLOCK)[:PAIRS])(keys)
    return picks.reshape(TILES, OFFSETS, PAIRS).astype(jnp.int32)


def draw_out_rows(key, part):
    key = jax.random.fold_in(key, 9)
    keys = jax.random.split(key, TILES * OFFSETS)
    picks = jax.vmap(lambda one_key: jax.random.permutation(one_key, TILE_BLOCKS * BLOCK)[:PAIRS])(keys)
    return picks.reshape(TILES, OFFSETS, PAIRS).astype(jnp.int32)


def draw_pair_count(key, part):
    key = jax.random.fold_in(key, 10)
    level_key, busy_key, spare_key, jitter_key = jax.random.split(key, 4)
    level = jax.random.randint(level_key, (TILES,), 1, 5)
    busy = jax.random.randint(busy_key, (), 0, TILES)
    spare = (busy + 1 + jax.random.randint(spare_key, (), 0, TILES - 1)) % TILES
    tile_ids = jnp.arange(TILES, dtype=jnp.int32)
    level = jnp.where(tile_ids == busy, 4, jnp.where(tile_ids == spare, 1, level))
    jitter = jax.random.randint(jitter_key, (TILES, OFFSETS), 0, PAIRS // 8)
    jitter = jitter.at[:, OFFSETS // 2].set(0)
    return (PAIRS // 4 * level[:, None] - jitter).astype(jnp.int32)


def level_of(stream_key, shape, shards, low, largest):
    loudness, own = 1.0, jax.random.fold_in(stream_key, 6)
    for position, shards_of in shards:
        heights = jnp.exp(jax.random.uniform(jax.random.fold_in(own, position), (shards_of,), jnp.float32, low / len(shards), largest / len(shards)))
        loudness = loudness * jnp.repeat(heights, shape[position] // shards_of).reshape([-1 if axis == position else 1 for axis in range(len(shape))])
    return loudness


def bell_draw(stream_key, dims, width, most, pieces=(), held_as=jnp.bfloat16):
    gain = level_of(stream_key, dims, pieces, -0.22, 0.18) if pieces else 1.0
    values = jax.random.normal(stream_key, dims, jnp.float32) * width * gain
    return jnp.minimum(jnp.maximum(values, -most), most).astype(held_as)


def setup_inputs(seed: int = 0, part: int = 0) -> dict:
    streams_of = jax.random.split(jax.random.key(seed), 10)
    own_keys = jax.random.split(jax.random.fold_in(streams_of[9], part), 10)
    return {
        "log_features": bell_draw(own_keys[0], (TILES, LOG_BLOCKS, CHANNELS, BLOCK), 0.5, 3.0, ((0, 8), (2, 2))),
        "send_slot": draw_send_slot(jax.random.fold_in(jax.random.fold_in(streams_of[9], part), 71), part),
        "merge_slot": draw_merge_slot(jax.random.fold_in(jax.random.fold_in(streams_of[9], part), 71), part),
        "halo_list": draw_halo_list(jax.random.fold_in(jax.random.fold_in(streams_of[9], part), 71), part),
        "in_rows": draw_in_rows(jax.random.fold_in(jax.random.fold_in(streams_of[9], part), 71), part),
        "out_rows": draw_out_rows(jax.random.fold_in(jax.random.fold_in(streams_of[9], part), 71), part),
        "pair_count": draw_pair_count(jax.random.fold_in(jax.random.fold_in(streams_of[9], part), 71), part),
        "weight": bell_draw(streams_of[7], (OFFSETS, CHANNELS, CHANNELS), (9 * CHANNELS) ** -0.5, 0.1875),
        "cotangent": bell_draw(own_keys[8], (TILES, TILE_BLOCKS, CHANNELS, BLOCK), 1.0, 6.0, ((0, 8), (2, 2))),
    }


def gather_rows(blocks, row_ids):
    return blocks[row_ids // BLOCK, :, row_ids % BLOCK]


def add_rows(blocks, row_ids, values):
    return blocks.at[row_ids // BLOCK, :, row_ids % BLOCK].add(values)


def relay_in(log_features, send_slot, merge_slot):
    flat_logs = log_features.reshape(TILES * LOG_BLOCKS, CHANNELS * BLOCK)

    def one_tile(tile_id):
        slot_table = lax.dynamic_index_in_dim(send_slot, tile_id, 1, keepdims=False)
        log_rows = jnp.arange(TILES, dtype=jnp.int32)[:, None] * LOG_BLOCKS + jnp.maximum(slot_table, 0)
        sent_blocks = flat_logs[log_rows.reshape(-1)]
        targets = lax.dynamic_index_in_dim(merge_slot, tile_id, 0, keepdims=False).reshape(-1)
        place_table = (jnp.arange(TILE_BLOCKS, dtype=jnp.int32)[:, None] == targets[None, :]).astype(jnp.bfloat16)
        return jnp.dot(place_table, sent_blocks, preferred_element_type=jnp.float32).astype(jnp.bfloat16)

    merged = lax.map(one_tile, jnp.arange(TILES, dtype=jnp.int32))
    return merged.reshape(TILES, TILE_BLOCKS, CHANNELS, BLOCK)


def neighbour_rim(features, halo_list, neighbour, direction, present):
    clamped = jnp.clip(neighbour, 0, TILES - 1)
    picked = features[clamped][halo_list[clamped, direction]]
    return jnp.where(present, picked, jnp.zeros_like(picked))


def returned_rim(rim_grads, neighbour, group, present):
    clamped = jnp.clip(neighbour, 0, TILES - 1)
    picked = rim_grads[clamped, group].astype(jnp.float32)
    return jnp.where(present, picked, jnp.zeros_like(picked))


def reference(log_features, send_slot, merge_slot, halo_list, in_rows, out_rows, pair_count, weight, cotangent):
    features = relay_in(log_features, send_slot, merge_slot)
    live_range = jnp.arange(PAIRS, dtype=jnp.int32)
    zero_block = jnp.zeros((1, CHANNELS, BLOCK), features.dtype)
    offset_ids = jnp.arange(OFFSETS, dtype=jnp.int32)

    def tile_pass(weight_total, tile_id):
        row_index = tile_id // DEPTHS
        column_index = tile_id % DEPTHS
        extended = jnp.concatenate([
            features[tile_id],
            neighbour_rim(features, halo_list, tile_id - DEPTHS, 1, row_index > 0),
            neighbour_rim(features, halo_list, tile_id + DEPTHS, 0, row_index < TILE_ROWS - 1),
            neighbour_rim(features, halo_list, tile_id - 1, 3, column_index > 0),
            neighbour_rim(features, halo_list, tile_id + 1, 2, column_index < DEPTHS - 1),
            zero_block], 0)
        live_mask = live_range[None, :] < pair_count[tile_id][:, None]
        source_rows = jnp.where(live_mask, in_rows[tile_id], EXT_BLOCKS * BLOCK)
        target_rows = jnp.where(live_mask, out_rows[tile_id], TILE_BLOCKS * BLOCK)

        def forward(running, offset):
            columns = gather_rows(extended, source_rows[offset])
            product = jnp.dot(columns, weight[offset], preferred_element_type=jnp.float32)
            return add_rows(running, target_rows[offset], product), None

        preact, _ = lax.scan(forward, jnp.zeros((TILE_BLOCKS + 1, CHANNELS, BLOCK), jnp.float32), offset_ids)
        preact = preact[:TILE_BLOCKS]
        activations = jax.nn.silu(preact).astype(jnp.bfloat16)
        sigmoid_pre = jax.nn.sigmoid(preact)
        grad_preact = (cotangent[tile_id].astype(jnp.float32) * sigmoid_pre * (1.0 + preact * (1.0 - sigmoid_pre))).astype(jnp.bfloat16)
        grad_padded = jnp.concatenate([grad_preact, zero_block.astype(grad_preact.dtype)], 0)

        def backward(grad_extended, offset):
            columns = gather_rows(extended, source_rows[offset])
            grad_columns = gather_rows(grad_padded, target_rows[offset])
            returned = jnp.dot(grad_columns, weight[offset].T, preferred_element_type=jnp.float32)
            weight_term = jnp.dot(columns.T, grad_columns, preferred_element_type=jnp.float32)
            return add_rows(grad_extended, source_rows[offset], returned), weight_term

        grad_extended, weight_terms = lax.scan(backward, jnp.zeros((EXT_BLOCKS + 1, CHANNELS, BLOCK), jnp.float32), offset_ids)
        rim_grads = grad_extended[TILE_BLOCKS:EXT_BLOCKS].astype(jnp.bfloat16).reshape(4, RIM_BLOCKS, CHANNELS, BLOCK)
        return weight_total + weight_terms, (activations, grad_extended[:TILE_BLOCKS], rim_grads)

    weight_total, outputs = lax.scan(tile_pass, jnp.zeros((OFFSETS, CHANNELS, CHANNELS), jnp.float32), jnp.arange(TILES, dtype=jnp.int32))
    activations, own_grads, rim_grads = outputs

    def finish(tile_id):
        row_index = tile_id // DEPTHS
        column_index = tile_id % DEPTHS
        rim_list = halo_list[tile_id]
        running = own_grads[tile_id]
        running = running.at[rim_list[0]].add(returned_rim(rim_grads, tile_id - DEPTHS, 1, row_index > 0))
        running = running.at[rim_list[1]].add(returned_rim(rim_grads, tile_id + DEPTHS, 0, row_index < TILE_ROWS - 1))
        running = running.at[rim_list[2]].add(returned_rim(rim_grads, tile_id - 1, 3, column_index > 0))
        running = running.at[rim_list[3]].add(returned_rim(rim_grads, tile_id + 1, 2, column_index < DEPTHS - 1))
        return running.astype(jnp.bfloat16)

    tile_grad = lax.map(finish, jnp.arange(TILES, dtype=jnp.int32))
    flat_grad = tile_grad.reshape(TILES, TILE_BLOCKS, CHANNELS * BLOCK)
    peer_ids = jnp.repeat(jnp.arange(TILES, dtype=jnp.int32), CAPACITY)

    def one_source(source_id):
        slot_table = send_slot[source_id].reshape(-1)
        targets = jnp.maximum(lax.dynamic_index_in_dim(merge_slot, source_id, 1, keepdims=False), 0).reshape(-1)
        back_blocks = flat_grad[peer_ids, targets]
        pick_table = (jnp.arange(LOG_BLOCKS, dtype=jnp.int32)[:, None] == slot_table[None, :]).astype(jnp.bfloat16)
        return jnp.dot(pick_table, back_blocks, preferred_element_type=jnp.float32).astype(jnp.bfloat16)

    grad_log = lax.map(one_source, jnp.arange(TILES, dtype=jnp.int32)).reshape(TILES, LOG_BLOCKS, CHANNELS, BLOCK)
    grad_weight = weight_total * (TILES * PAIRS) ** -0.5
    return activations, grad_log, grad_weight
```

```python
import functools

import jax
import jax.numpy as jnp
from jax import lax
from jax.experimental import pallas as pl
from jax.experimental.pallas import tpu as pltpu
from jax.sharding import PartitionSpec as P

F32 = jnp.float32
BF16 = jnp.bfloat16
TILES_AXES = ("tile", "depth")
VMEM = pl.BlockSpec(memory_space=pltpu.VMEM)
SMEM = pl.BlockSpec(memory_space=pltpu.SMEM)
PARAMS = pltpu.CompilerParams(vmem_limit_bytes=24 * 1024 * 1024)


def shape(dims, dtype):
    return jax.ShapeDtypeStruct(dims, dtype)


def pair_lists(size):
    return [
        [pair for i in range(first, size - 1, 2) for pair in ((i, i + 1), (i + 1, i))]
        for first in (0, 1)
    ]


def exchanges(tile_rows, depths):
    found = []
    for axis, size in (("tile", tile_rows), ("depth", depths)):
        for parity, pairs in enumerate(pair_lists(size)):
            if pairs:
                found.append((axis, parity, pairs))
    return found


def direction(axis, parity):
    place = lax.axis_index(axis) % 2
    upper = (place == parity).astype(jnp.int32)
    return upper + (0 if axis == "tile" else 2)


def xor_pairs(size, distance):
    return [(i, i ^ distance) for i in range(size)]


def premerge_kernel(tile_rows, depths, tile_blocks, *refs):
    send_ref, own_ref = refs[0], refs[1]
    near = refs[2 : 2 + tile_rows - 1]
    far = refs[2 + tile_rows - 1 : 2 + tile_rows - 1 + depths - 1]
    log_ref, out_ref, place_ref = refs[-3:]
    log_count, half, width = log_ref.shape
    capacity = send_ref.shape[1]
    i, j = lax.axis_index("tile"), lax.axis_index("depth")
    me = i * depths + j
    for jx in range(depths):
        for d in range(tile_rows):
            p = (i ^ d) * depths + (j ^ jx)
            q = jx * tile_rows + d
            totals = [jnp.zeros((half, width), F32) for _ in range(tile_blocks)]
            for c in range(capacity):
                block = send_ref[p, c]
                if jx:
                    target = far[jx - 1][d, me, c]
                elif d:
                    target = near[d - 1][me, c]
                else:
                    target = own_ref[me, c]
                live = block >= 0
                place_ref[jnp.where(live, block, log_count)] = q * tile_blocks + target
                rows = log_ref[jnp.maximum(block, 0)].astype(F32)
                wanted = jnp.where(live, target, -1)
                for m in range(tile_blocks):
                    totals[m] = totals[m] + rows * jnp.where(wanted == m, 1.0, 0.0)
            for m in range(tile_blocks):
                out_ref[p * tile_blocks + m] = totals[m].astype(BF16)


def merge_kernel(swaps, incoming_ref, halo_ref, features_ref, *sends):
    sources, tile_blocks = incoming_ref.shape[:2]
    for m in range(tile_blocks):
        total = incoming_ref[0, m].astype(F32)
        for s in range(1, sources):
            total = total + incoming_ref[s, m].astype(F32)
        features_ref[m] = total.astype(BF16)
    pick_blocks(swaps, features_ref, halo_ref, sends)


def pick_blocks(swaps, features_ref, halo_ref, sends):
    for (axis, parity, _), send_ref in zip(swaps, sends):
        group = direction(axis, parity)
        for b in range(send_ref.shape[0]):
            send_ref[b] = features_ref[halo_ref[group, b]]


def table_row(ref, k):
    return ref[k : k + 1, :]


def one_hot(low, height):
    rows = lax.broadcasted_iota(jnp.int32, (height, low.shape[1]), 0)
    return jnp.where(rows == low, 1.0, 0.0).astype(BF16)


def forward_kernel(swap_count, chunk, *refs):
    features_ref = refs[0]
    received = refs[1 : 1 + swap_count]
    source_ref, target_ref, weight_ref = refs[1 + swap_count : 4 + swap_count]
    part_ref, columns_ref, values, places = refs[4 + swap_count :]
    tile_blocks, half, width = features_ref.shape
    offsets = weight_ref.shape[0]
    channels = weight_ref.shape[1]
    span = 2 * width
    blocks = [features_ref[b] for b in range(tile_blocks)]
    for ref in received:
        blocks += [ref[b] for b in range(ref.shape[0])]
    folds = len(blocks) // 2
    folded = jnp.concatenate(
        [jnp.concatenate([blocks[2 * f], blocks[2 * f + 1]], 1) for f in range(folds)], 0
    )
    for first in range(0, offsets, chunk):
        ks = range(first, first + chunk)
        rows = [table_row(source_ref, k) for k in ks]
        table = jnp.concatenate([one_hot(r & (span - 1), span) for r in rows], 1)
        gathered = jnp.dot(folded, table, preferred_element_type=F32)
        for n, k in enumerate(ks):
            lanes = slice(n * width, (n + 1) * width)
            fold = rows[n] // span
            picked = jnp.zeros((half, width), F32)
            for f in range(folds):
                picked = jnp.where(fold == f, gathered[f * half : (f + 1) * half, lanes], picked)
            picked = picked.astype(BF16)
            columns_ref[:, k * width : (k + 1) * width] = picked
            product = jnp.dot(weight_ref[k], picked, preferred_element_type=F32)
            target = table_row(target_ref, k)
            fold = target // span
            places[:, k * width : (k + 1) * width] = one_hot(target & (span - 1), span)
            for f in range(2):
                values[f * channels : (f + 1) * channels, k * width : (k + 1) * width] = jnp.where(
                    fold == f, product, 0.0
                ).astype(BF16)
    total = lax.dot_general(
        values[...], places[...], (((1,), (1,)), ((), ())), preferred_element_type=F32
    )
    part_ref[:, :span] = total[:channels]
    part_ref[:, span:] = total[channels:]


def activation_kernel(chunk, *refs):
    part_ref, other_ref, cotangent_ref, target_ref, columns_ref = refs[:5]
    act_ref, weight_grad_ref, grad_columns_ref = refs[5:]
    tile_blocks, channels, width = cotangent_ref.shape
    half = columns_ref.shape[0]
    offsets = weight_grad_ref.shape[0] // half
    span = 2 * width
    start = pl.multiple_of(lax.axis_index("chan") * half, half)
    own = part_ref[pl.ds(start, half), :] + other_ref[pl.ds(start, half), :]
    own = own / (1.0 + jnp.exp(-own))
    for b in range(tile_blocks):
        act_ref[b] = own[:, b * width : (b + 1) * width].astype(BF16)
    preact = part_ref[...] + other_ref[...]
    gate = 1.0 / (1.0 + jnp.exp(-preact))
    cotangent = jnp.concatenate([cotangent_ref[b] for b in range(tile_blocks)], 1).astype(F32)
    grad = (cotangent * gate * (1.0 + preact * (1.0 - gate))).astype(BF16)
    folded = jnp.concatenate([grad[:, :span], grad[:, span:]], 0)
    for first in range(0, offsets, chunk):
        ks = range(first, first + chunk)
        rows = [table_row(target_ref, k) for k in ks]
        table = jnp.concatenate([one_hot(r & (span - 1), span) for r in rows], 1)
        gathered = jnp.dot(folded, table, preferred_element_type=F32)
        for n, k in enumerate(ks):
            lanes = slice(n * width, (n + 1) * width)
            fold = rows[n] // span
            picked = jnp.where(
                fold == 0,
                gathered[:channels, lanes],
                jnp.where(fold == 1, gathered[channels:, lanes], 0.0),
            ).astype(BF16)
            grad_columns_ref[:, k * width : (k + 1) * width] = picked
            term = lax.dot_general(
                columns_ref[:, k * width : (k + 1) * width],
                picked,
                (((1,), (1,)), ((), ())),
                preferred_element_type=F32,
            )
            weight_grad_ref[k * half : (k + 1) * half, :] = term.astype(weight_grad_ref.dtype)


def input_grad_kernel(tile_blocks, grad_columns_ref, source_ref, weight_ref, own_ref, *refs):
    rims, (values, places) = refs[:-2], refs[-2:]
    offsets, half, _ = weight_ref.shape
    width = source_ref.shape[1]
    span = 2 * width
    folds = values.shape[0] // half
    for k in range(offsets):
        lanes = slice(k * width, (k + 1) * width)
        source = table_row(source_ref, k)
        fold = source // span
        returned = jnp.dot(weight_ref[k], grad_columns_ref[:, lanes], preferred_element_type=F32)
        places[:, lanes] = one_hot(source & (span - 1), span)
        for f in range(folds):
            values[f * half : (f + 1) * half, lanes] = jnp.where(fold == f, returned, 0.0).astype(
                BF16
            )
    total = lax.dot_general(
        values[...], places[...], (((1,), (1,)), ((), ())), preferred_element_type=F32
    )

    def block(b):
        return total[(b // 2) * half : (b // 2 + 1) * half, (b % 2) * width : (b % 2 + 1) * width]

    for b in range(tile_blocks):
        own_ref[b] = block(b)
    place = tile_blocks
    for rim in rims:
        for b in range(rim.shape[0]):
            rim[b] = block(place).astype(BF16)
            place += 1


def tile_grad_kernel(swaps, own_ref, halo_ref, *refs):
    received, (out_ref, total) = refs[:-2], refs[-2:]
    total[...] = own_ref[...]
    for (axis, parity, _), ref in zip(swaps, received):
        group = direction(axis, parity)
        for b in range(ref.shape[0]):
            where = halo_ref[group, b]
            total[where] = total[where] + ref[b].astype(F32)
    out_ref[...] = total[...].astype(BF16)


def spread_kernel(place_ref, *refs):
    parts, (out_ref, held) = refs[:-2], refs[-2:]
    first = 0
    for ref in parts:
        count = ref.shape[0]
        held[first : first + count] = ref[...]
        first += count
    for b in range(out_ref.shape[0]):
        out_ref[b] = held[place_ref[b]]


def weight_kernel(tile_rows, depths, scale, *refs):
    parts, (out_ref, held) = refs[:-2], refs[-2:]
    i, j = lax.axis_index("tile"), lax.axis_index("depth")
    rows = parts[0].shape[0]
    for jx in range(depths):
        for d in range(tile_rows):
            p = (i ^ d) * depths + (j ^ jx)
            start = pl.multiple_of(p * rows, rows)
            held[pl.ds(start, rows), :] = parts[jx * tile_rows + d][...].astype(F32) * scale
    out_ref[...] = held[: out_ref.shape[0], :]


def swap_all(swaps, arrays):
    return [
        lax.ppermute(array, axis, pairs) for (axis, _, pairs), array in zip(swaps, arrays)
    ]


def share(own, tile_rows, depths):
    near = [own] + [
        lax.ppermute(own, "tile", xor_pairs(tile_rows, d)) for d in range(1, tile_rows)
    ]
    found = list(near)
    for jx in range(1, depths):
        found += [lax.ppermute(part, "depth", xor_pairs(depths, jx)) for part in near]
    return found


def relay(outgoing):
    return lax.all_to_all(outgoing, TILES_AXES, split_axis=0, concat_axis=0, tiled=True)


def local(
    log_features, send_slot, merge_slot, halo_list, in_rows, out_rows, pair_count, weight, cotangent
):
    tile_rows = lax.axis_size("tile")
    depths = lax.axis_size("depth")
    tile_count = tile_rows * depths
    log_blocks = log_features[0]
    log_count, half, width = log_blocks.shape
    tile_blocks = cotangent.shape[1]
    offsets, channels, _ = weight.shape
    capacity = send_slot.shape[2]
    rim_count = halo_list.shape[2]
    pair_slots = in_rows.shape[2]
    own_total = tile_blocks * width
    span = 2 * width
    chunk = 4
    padded = -(-offsets // chunk) * chunk
    swaps = exchanges(tile_rows, depths)
    powers = all(n & (n - 1) == 0 for n in (tile_rows, depths))
    merged = powers and tile_count <= 8 and capacity >= tile_blocks
    send, merge, halo = send_slot[0], merge_slot[0], halo_list[0]

    block_of = in_rows[0] // width
    group_of = (block_of - tile_blocks) // rim_count
    held_total = tile_blocks + len(swaps) * rim_count
    new_block = jnp.where(block_of < tile_blocks, block_of, held_total)
    for place, (axis, parity, _) in enumerate(swaps):
        hit = (block_of >= tile_blocks) & (group_of == direction(axis, parity))
        inside = (block_of - tile_blocks) % rim_count
        new_block = jnp.where(hit, tile_blocks + place * rim_count + inside, new_block)
    live = jnp.arange(pair_slots, dtype=jnp.int32)[None, :] < pair_count[0][:, None]
    source_rows = jnp.where(live, new_block * width + in_rows[0] % width, held_total * width)
    target_rows = jnp.where(live, out_rows[0], own_total)
    extra = ((0, padded - offsets), (0, 0))
    source_rows = jnp.pad(source_rows, extra, constant_values=held_total * width)
    target_rows = jnp.pad(target_rows, extra, constant_values=own_total)
    w_rows = lax.dynamic_slice_in_dim(weight, lax.axis_index("chan") * half, half, 1)
    w_rows = jnp.pad(w_rows, ((0, padded - offsets), (0, 0), (0, 0)))
    w_rows_t = w_rows.transpose(0, 2, 1)
    cotangent_full = lax.all_gather(cotangent[0], "chan", axis=1, tiled=True)

    rim_shape = shape((rim_count, half, width), BF16)
    block_shape = shape((tile_blocks, half, width), BF16)
    if merged:
        near = [merge] + [
            lax.ppermute(merge, "tile", xor_pairs(tile_rows, d)) for d in range(1, tile_rows)
        ]
        stacked = jnp.stack(near)
        far = [
            lax.ppermute(stacked, "depth", xor_pairs(depths, jx)) for jx in range(1, depths)
        ]
        outgoing, place = pl.pallas_call(
            functools.partial(premerge_kernel, tile_rows, depths, tile_blocks),
            out_shape=(
                shape((tile_count * tile_blocks, half, width), BF16),
                shape((log_count + 1,), jnp.int32),
            ),
            in_specs=[SMEM] * (1 + len(near) + len(far)) + [VMEM],
            out_specs=(VMEM, SMEM),
            compiler_params=PARAMS,
        )(send, *near, *far, log_blocks)
        incoming = relay(outgoing.reshape(tile_count, tile_blocks, half, width))
    else:
        pick_table = (
            send.reshape(-1)[:, None] == jnp.arange(log_count, dtype=jnp.int32)[None, :]
        ).astype(BF16)
        outgoing = jnp.dot(
            pick_table, log_blocks.reshape(log_count, half * width), preferred_element_type=F32
        ).astype(BF16)
        incoming = relay(outgoing.reshape(tile_count, capacity, half, width))
        place_table = (
            jnp.arange(tile_blocks, dtype=jnp.int32)[:, None] == merge.reshape(-1)[None, :]
        ).astype(BF16)
        incoming = jnp.dot(
            place_table,
            incoming.reshape(tile_count * capacity, half * width),
            preferred_element_type=F32,
        )
        incoming = incoming.astype(BF16).reshape(1, tile_blocks, half, width)
    features, *sends = pl.pallas_call(
        functools.partial(merge_kernel, swaps),
        out_shape=(block_shape,) + (rim_shape,) * len(swaps),
        in_specs=[VMEM, SMEM],
        out_specs=(VMEM,) * (1 + len(swaps)),
        compiler_params=PARAMS,
    )(incoming, halo)
    received = swap_all(swaps, sends)

    pairs_total = padded * pair_slots
    part, columns = pl.pallas_call(
        functools.partial(forward_kernel, len(swaps), chunk),
        out_shape=(shape((channels, own_total), F32), shape((half, pairs_total), BF16)),
        in_specs=[VMEM] * (4 + len(swaps)),
        out_specs=(VMEM, VMEM),
        scratch_shapes=[
            pltpu.VMEM((2 * channels, pairs_total), BF16),
            pltpu.VMEM((span, pairs_total), BF16),
        ],
        compiler_params=PARAMS,
    )(features, *received, source_rows, target_rows, w_rows_t)
    other = lax.ppermute(part, "chan", [(0, 1), (1, 0)])

    weight_type = BF16 if merged else F32
    activations, weight_terms, grad_columns = pl.pallas_call(
        functools.partial(activation_kernel, chunk),
        out_shape=(
            block_shape,
            shape((padded * half, channels), weight_type),
            shape((channels, pairs_total), BF16),
        ),
        in_specs=[VMEM] * 5,
        out_specs=(VMEM,) * 3,
        compiler_params=PARAMS,
    )(part, other, cotangent_full, target_rows, columns)

    scale = float(tile_count * pair_slots) ** (-0.5)
    if merged:
        shards = relay(weight_terms.reshape(tile_count, -1, channels))
    own_grad, *rims = pl.pallas_call(
        functools.partial(input_grad_kernel, tile_blocks),
        out_shape=(shape((tile_blocks, half, width), F32),) + (rim_shape,) * len(swaps),
        in_specs=[VMEM] * 3,
        out_specs=(VMEM,) * (1 + len(swaps)),
        scratch_shapes=[
            pltpu.VMEM((held_total // 2 * half, pairs_total), BF16),
            pltpu.VMEM((span, pairs_total), BF16),
        ],
        compiler_params=PARAMS,
    )(grad_columns, source_rows, w_rows)
    returned = swap_all(swaps, rims)
    tile_grad = pl.pallas_call(
        functools.partial(tile_grad_kernel, swaps),
        out_shape=block_shape,
        in_specs=[VMEM, SMEM] + [VMEM] * len(swaps),
        out_specs=VMEM,
        scratch_shapes=[pltpu.VMEM((tile_blocks, half, width), F32)],
        compiler_params=PARAMS,
    )(own_grad, halo, *returned)

    if merged:
        parts = share(tile_grad, tile_rows, depths)
        grad_log = pl.pallas_call(
            spread_kernel,
            out_shape=shape((log_count, half, width), BF16),
            in_specs=[SMEM] + [VMEM] * len(parts),
            out_specs=VMEM,
            scratch_shapes=[pltpu.VMEM((tile_count * tile_blocks, half, width), BF16)],
            compiler_params=PARAMS,
        )(place, *parts)
        shard = shards.astype(F32).sum(0).astype(BF16)
        shares = share(shard, tile_rows, depths)
        grad_weight = pl.pallas_call(
            functools.partial(weight_kernel, tile_rows, depths, scale),
            out_shape=shape((offsets * half, channels), F32),
            in_specs=[VMEM] * len(shares),
            out_specs=VMEM,
            scratch_shapes=[pltpu.VMEM((padded * half, channels), F32)],
            compiler_params=PARAMS,
        )(*shares)
    else:
        back_blocks = jnp.dot(
            place_table.T,
            tile_grad.reshape(tile_blocks, half * width),
            preferred_element_type=F32,
        ).astype(BF16)
        back = relay(back_blocks.reshape(tile_count, capacity, half, width))
        grad_log = jnp.dot(
            pick_table.T,
            back.reshape(tile_count * capacity, half * width),
            preferred_element_type=F32,
        ).astype(BF16)
        grad_weight = lax.psum(weight_terms[: offsets * half], TILES_AXES) * scale
    return (
        activations[None],
        grad_log.reshape(1, log_count, half, width),
        grad_weight.reshape(offsets, half, channels),
    )


def solution(mesh):
    split = ("groups", "tile", "depth")
    in_specs = (
        P(split, None, "chan", None),
        P(split, None, None),
        P(split, None, None),
        P(split, None, None),
        P(split, None, None),
        P(split, None, None),
        P(split, None),
        P(),
        P(split, None, "chan", None),
    )
    out_specs = (
        P(split, None, "chan", None),
        P(split, None, "chan", None),
        P("groups", "chan", None),
    )
    return jax.shard_map(local, mesh=mesh, in_specs=in_specs, out_specs=out_specs, check_vma=False)
```

```python
import functools

import jax
import jax.numpy as jnp
from jax import lax
from jax.experimental import pallas as pl
from jax.experimental.pallas import tpu as pltpu
from jax.sharding import PartitionSpec as P

F32 = jnp.float32
BF16 = jnp.bfloat16
TILES_AXES = ("tile", "depth")
VMEM = pl.BlockSpec(memory_space=pltpu.VMEM)
SMEM = pl.BlockSpec(memory_space=pltpu.SMEM)
PARAMS = pltpu.CompilerParams(vmem_limit_bytes=24 * 1024 * 1024)


def shape(dims, dtype):
    return jax.ShapeDtypeStruct(dims, dtype)


def pair_lists(size):
    return [
        [pair for i in range(first, size - 1, 2) for pair in ((i, i + 1), (i + 1, i))]
        for first in (0, 1)
    ]


def exchanges(tile_rows, depths):
    found = []
    for axis, size in (("tile", tile_rows), ("depth", depths)):
        for parity, pairs in enumerate(pair_lists(size)):
            if pairs:
                found.append((axis, parity, pairs))
    return found


def direction(axis, parity):
    place = lax.axis_index(axis) % 2
    upper = (place == parity).astype(jnp.int32)
    return upper + (0 if axis == "tile" else 2)


def xor_pairs(size, distance):
    return [(i, i ^ distance) for i in range(size)]


def merge_column(jx, rows_away, depths, tile_blocks, send_ref, tables, log_ref, emit):
    i, j = lax.axis_index("tile"), lax.axis_index("depth")
    me = i * depths + j
    half, width = log_ref.shape[1:]
    for d in rows_away:
        p = (i ^ d) * depths + (j ^ jx)
        totals = [jnp.zeros((half, width), F32) for _ in range(tile_blocks)]
        for c in range(send_ref.shape[1]):
            block = send_ref[p, c]
            wanted = jnp.where(block >= 0, tables(d, me, c), -1)
            rows = log_ref[jnp.maximum(block, 0)].astype(F32)
            for m in range(tile_blocks):
                totals[m] = totals[m] + rows * jnp.where(wanted == m, 1.0, 0.0)
        for m in range(tile_blocks):
            emit(d, m, totals[m])


def copy_kernel(in_ref, out_ref):
    out_ref[...] = in_ref[...]


def far_kernel(rows_away, depths, tile_blocks, send_ref, far_ref, log_ref, out_ref):
    def emit(d, m, total):
        out_ref[(d - rows_away[0]) * tile_blocks + m] = total.astype(BF16)

    merge_column(
        1, rows_away, depths, tile_blocks, send_ref, lambda *at: far_ref[at], log_ref, emit
    )


def near_kernel(tile_rows, depths, tile_blocks, *refs):
    send_ref, tables, far_ref = refs[0], refs[1 : 1 + tile_rows], refs[1 + tile_rows]
    log_ref, (*outs, place_ref) = refs[2 + tile_rows], refs[3 + tile_rows :]
    per = tile_rows // len(outs)
    i, j = lax.axis_index("tile"), lax.axis_index("depth")
    me = i * depths + j

    def emit(d, m, total):
        outs[d // per][(d % per) * tile_blocks + m] = total

    merge_column(
        0,
        range(tile_rows),
        depths,
        tile_blocks,
        send_ref,
        lambda d, *at: tables[d][at],
        log_ref,
        emit,
    )
    for jx in range(depths):
        for d in range(tile_rows):
            p = (i ^ d) * depths + (j ^ jx)
            for c in range(send_ref.shape[1]):
                block = send_ref[p, c]
                target = far_ref[d, me, c] if jx else tables[d][me, c]
                spot = jnp.where(block >= 0, block, log_ref.shape[0])
                place_ref[spot] = (jx * tile_rows + d) * tile_blocks + target


def add_kernel(near_ref, far_ref, *outs):
    count = near_ref.shape[0] // len(outs)
    for n, ref in enumerate(outs):
        for m in range(count):
            at = n * count + m
            ref[m] = (near_ref[at] + far_ref[at].astype(F32)).astype(ref.dtype)


def merge_kernel(swaps, halo_ref, *refs):
    incoming, features_ref = refs[: -1 - len(swaps)], refs[-1 - len(swaps)]
    sends = refs[-len(swaps) :] if swaps else ()
    for m in range(features_ref.shape[0]):
        total = incoming[0][m].astype(F32)
        for ref in incoming[1:]:
            total = total + ref[m].astype(F32)
        features_ref[m] = total.astype(BF16)
    pick_blocks(swaps, features_ref, halo_ref, sends)


def pick_blocks(swaps, features_ref, halo_ref, sends):
    for (axis, parity, _), send_ref in zip(swaps, sends):
        group = direction(axis, parity)
        for b in range(send_ref.shape[0]):
            send_ref[b] = features_ref[halo_ref[group, b]]


def table_row(ref, k):
    return ref[k : k + 1, :]


def one_hot(low, height):
    rows = lax.broadcasted_iota(jnp.int32, (height, low.shape[1]), 0).astype(F32).astype(BF16)
    low = low.astype(F32).astype(BF16)
    return jnp.where(rows == low, jnp.ones((), BF16), jnp.zeros((), BF16))


def pick_fold(fold, parts):
    picked = jnp.zeros_like(parts[0])
    for f, part in enumerate(parts):
        picked = jnp.where(fold == f, part, picked)
    return picked


def mask_fold(fold, f, part):
    return jnp.where(fold == f, part, jnp.zeros_like(part))


def forward_kernel(swap_count, chunk, *refs):
    features_ref = refs[0]
    received = refs[1 : 1 + swap_count]
    source_ref, target_ref, weight_ref = refs[1 + swap_count : 4 + swap_count]
    part_ref, columns_ref, values, places = refs[4 + swap_count :]
    tile_blocks, half, width = features_ref.shape
    offsets = weight_ref.shape[0]
    channels = weight_ref.shape[1]
    span = 2 * width
    blocks = [features_ref[b] for b in range(tile_blocks)]
    for ref in received:
        blocks += [ref[b] for b in range(ref.shape[0])]
    folds = len(blocks) // 2
    folded = jnp.concatenate(
        [jnp.concatenate([blocks[2 * f], blocks[2 * f + 1]], 1) for f in range(folds)], 0
    )
    for first in range(0, offsets, chunk):
        ks = range(first, first + chunk)
        rows = [table_row(source_ref, k) for k in ks]
        table = jnp.concatenate([one_hot(r & (span - 1), span) for r in rows], 1)
        gathered = jnp.dot(folded, table, preferred_element_type=F32).astype(BF16)
        for n, k in enumerate(ks):
            lanes = slice(n * width, (n + 1) * width)
            fold = (rows[n] // span).astype(F32).astype(BF16)
            picked = pick_fold(
                fold, [gathered[f * half : (f + 1) * half, lanes] for f in range(folds)]
            )
            columns_ref[:, k * width : (k + 1) * width] = picked
            product = jnp.dot(weight_ref[k], picked, preferred_element_type=F32)
            product = product.astype(BF16)
            target = table_row(target_ref, k)
            fold = (target // span).astype(F32).astype(BF16)
            places[:, k * width : (k + 1) * width] = one_hot(target & (span - 1), span)
            for f in range(2):
                values[f * channels : (f + 1) * channels, k * width : (k + 1) * width] = mask_fold(
                    fold, f, product
                )
    total = lax.dot_general(
        values[...], places[...], (((1,), (1,)), ((), ())), preferred_element_type=F32
    )
    part_ref[:, :span] = total[:channels]
    part_ref[:, span:] = total[channels:]


def input_grad_kernel(chunk, *refs):
    part_ref, other_ref, cotangent_ref, source_ref, target_ref, weight_ref = refs[:6]
    grad_columns_ref, own_ref = refs[6:8]
    rims, (values, places) = refs[8:-2], refs[-2:]
    tile_blocks, channels, width = cotangent_ref.shape
    offsets, half, _ = weight_ref.shape
    span = 2 * width
    folds = values.shape[0] // half
    preact = part_ref[...] + other_ref[...]
    gate = 1.0 / (1.0 + jnp.exp(-preact))
    cotangent = jnp.concatenate([cotangent_ref[b] for b in range(tile_blocks)], 1).astype(F32)
    grad = (cotangent * gate * (1.0 + preact * (1.0 - gate))).astype(BF16)
    folded = jnp.concatenate([grad[:, :span], grad[:, span:]], 0)
    for first in range(0, offsets, chunk):
        ks = range(first, first + chunk)
        rows = [table_row(target_ref, k) for k in ks]
        table = jnp.concatenate([one_hot(r & (span - 1), span) for r in rows], 1)
        gathered = jnp.dot(folded, table, preferred_element_type=F32).astype(BF16)
        for n, k in enumerate(ks):
            inside = slice(n * width, (n + 1) * width)
            lanes = slice(k * width, (k + 1) * width)
            fold = (rows[n] // span).astype(F32).astype(BF16)
            picked = pick_fold(fold, [gathered[:channels, inside], gathered[channels:, inside]])
            grad_columns_ref[:, lanes] = picked
            returned = jnp.dot(weight_ref[k], picked, preferred_element_type=F32).astype(BF16)
            source = table_row(source_ref, k)
            fold = (source // span).astype(F32).astype(BF16)
            places[:, lanes] = one_hot(source & (span - 1), span)
            for f in range(folds):
                values[f * half : (f + 1) * half, lanes] = mask_fold(fold, f, returned)
    total = lax.dot_general(
        values[...], places[...], (((1,), (1,)), ((), ())), preferred_element_type=F32
    )

    def block(b):
        return total[(b // 2) * half : (b // 2 + 1) * half, (b % 2) * width : (b % 2 + 1) * width]

    for b in range(tile_blocks):
        own_ref[b] = block(b)
    place = tile_blocks
    for rim in rims:
        for b in range(rim.shape[0]):
            rim[b] = block(place).astype(BF16)
            place += 1


def weight_grad_kernel(part_ref, other_ref, columns_ref, grad_columns_ref, act_ref, *refs):
    portions, held = refs[:-1], refs[-1]
    half = columns_ref.shape[0]
    tile_blocks, _, width = act_ref.shape
    offsets = columns_ref.shape[1] // width
    portion = offsets // len(portions)
    here = lax.axis_index("depth") if len(portions) > 1 else 0
    for k in range(offsets):
        lanes = slice(k * width, (k + 1) * width)
        term = lax.dot_general(
            columns_ref[:, lanes],
            grad_columns_ref[:, lanes],
            (((1,), (1,)), ((), ())),
            preferred_element_type=F32,
        )
        row = (k % portion) * half
        held[(k // portion) ^ here, row : row + half, :] = term
    for n, ref in enumerate(portions):
        ref[...] = held[n].astype(ref.dtype)
    start = pl.multiple_of(lax.axis_index("chan") * half, half)
    own = part_ref[pl.ds(start, half), :] + other_ref[pl.ds(start, half), :]
    own = own / (1.0 + jnp.exp(-own))
    for b in range(tile_blocks):
        act_ref[b] = own[:, b * width : (b + 1) * width].astype(BF16)


def tile_grad_kernel(swaps, halo_ref, own_ref, *refs):
    received, (out_ref, total) = refs[:-2], refs[-2:]
    total[...] = own_ref[...]
    for (axis, parity, _), ref in zip(swaps, received):
        group = direction(axis, parity)
        for b in range(ref.shape[0]):
            where = halo_ref[group, b]
            total[where] = total[where] + ref[b].astype(F32)
    out_ref[...] = total[...].astype(BF16)


def row_sum_kernel(keep_ref, crossed_ref, *refs):
    outs, total = refs[:-1], refs[-1]
    total[...] = keep_ref[...] + crossed_ref[...].astype(F32)
    i = lax.axis_index("tile")
    rows = outs[0].shape[0]
    for d, ref in enumerate(outs):
        start = pl.multiple_of((i ^ d) * rows, rows)
        ref[...] = total[pl.ds(start, rows), :].astype(ref.dtype)


def column_kernel(tile_rows, *refs):
    grads, terms, (bulk_ref, shard_ref) = refs[:tile_rows], refs[tile_rows:-2], refs[-2:]
    row = 0
    for ref in grads:
        for b in range(ref.shape[0]):
            bulk_ref[row : row + ref.shape[1], :] = ref[b]
            row += ref.shape[1]
    total = terms[0][...]
    for ref in terms[1:]:
        total = total + ref[...].astype(F32)
    shard_ref[...] = total.astype(BF16)
    bulk_ref[row:, :] = shard_ref[...]


def row_sum_kernel(keep_ref, crossed_ref, *refs):
    outs, total = refs[:-1], refs[-1]
    total[...] = keep_ref[...] + crossed_ref[...].astype(F32)
    i = lax.axis_index("tile")
    rows = outs[0].shape[0]
    for d, ref in enumerate(outs):
        start = pl.multiple_of((i ^ d) * rows, rows)
        ref[...] = total[pl.ds(start, rows), :].astype(ref.dtype)


def column_kernel(tile_rows, *refs):
    grads, terms, (bulk_ref, shard_ref) = refs[:tile_rows], refs[tile_rows:-2], refs[-2:]
    row = 0
    for ref in grads:
        for b in range(ref.shape[0]):
            bulk_ref[row : row + ref.shape[1], :] = ref[b]
            row += ref.shape[1]
    total = terms[0][...]
    for ref in terms[1:]:
        total = total + ref[...].astype(F32)
    shard_ref[...] = total.astype(BF16)
    bulk_ref[row:, :] = shard_ref[...]


def spread_kernel(place_ref, own_ref, other_ref, out_ref, held):
    rows = held.shape[0] // 2
    height = out_ref.shape[1]
    held[:rows, :] = own_ref[:rows, :]
    held[rows:, :] = other_ref[:rows, :]
    for b in range(out_ref.shape[0]):
        first = pl.multiple_of(place_ref[b] * height, height)
        out_ref[b] = held[pl.ds(first, height), :]


def weight_kernel(scale, tile_rows, *refs):
    near, (bulk_ref, far_ref, out_ref, held) = refs[:tile_rows], refs[tile_rows:]
    i, j = lax.axis_index("tile"), lax.axis_index("depth")
    rows = near[0].shape[0]
    for jx in range(2):
        for d in range(tile_rows):
            if jx == 0:
                shard = near[d][...]
            elif d == 0:
                shard = bulk_ref[bulk_ref.shape[0] - rows :, :]
            else:
                shard = far_ref[(d - 1) * rows : d * rows, :]
            start = pl.multiple_of(((j ^ jx) * tile_rows + (i ^ d)) * rows, rows)
            held[pl.ds(start, rows), :] = shard.astype(F32) * scale
    out_ref[...] = held[: out_ref.shape[0], :]


def swap_all(swaps, arrays):
    return [
        lax.ppermute(array, axis, pairs) for (axis, _, pairs), array in zip(swaps, arrays)
    ]


def to_rows(arrays, tile_rows):
    return [arrays[0]] + [
        lax.ppermute(arrays[d], "tile", xor_pairs(tile_rows, d)) for d in range(1, tile_rows)
    ]


def across(array):
    return lax.ppermute(array, "depth", [(0, 1), (1, 0)])


def relay(outgoing):
    return lax.all_to_all(outgoing, TILES_AXES, split_axis=0, concat_axis=0, tiled=True)


def local(
    log_features, send_slot, merge_slot, halo_list, in_rows, out_rows, pair_count, weight, cotangent
):
    tile_rows = lax.axis_size("tile")
    depths = lax.axis_size("depth")
    tile_count = tile_rows * depths
    log_blocks = log_features[0]
    log_count, half, width = log_blocks.shape
    tile_blocks = cotangent.shape[1]
    offsets, channels, _ = weight.shape
    capacity = send_slot.shape[2]
    rim_count = halo_list.shape[2]
    pair_slots = in_rows.shape[2]
    own_total = tile_blocks * width
    span = 2 * width
    chunk = 4
    padded = -(-offsets // chunk) * chunk
    swaps = exchanges(tile_rows, depths)
    merged = (tile_rows, depths) == (4, 2) and capacity >= tile_blocks
    send, merge, halo = send_slot[0], merge_slot[0], halo_list[0]

    block_of = in_rows[0] // width
    group_of = (block_of - tile_blocks) // rim_count
    held_total = tile_blocks + len(swaps) * rim_count
    new_block = jnp.where(block_of < tile_blocks, block_of, held_total)
    for place, (axis, parity, _) in enumerate(swaps):
        hit = (block_of >= tile_blocks) & (group_of == direction(axis, parity))
        inside = (block_of - tile_blocks) % rim_count
        new_block = jnp.where(hit, tile_blocks + place * rim_count + inside, new_block)
    live = jnp.arange(pair_slots, dtype=jnp.int32)[None, :] < pair_count[0][:, None]
    source_rows = jnp.where(live, new_block * width + in_rows[0] % width, held_total * width)
    target_rows = jnp.where(live, out_rows[0], own_total)
    extra = ((0, padded - offsets), (0, 0))
    source_rows = jnp.pad(source_rows, extra, constant_values=held_total * width)
    target_rows = jnp.pad(target_rows, extra, constant_values=own_total)
    w_rows = lax.dynamic_slice_in_dim(weight, lax.axis_index("chan") * half, half, 1)
    w_rows = jnp.pad(w_rows, ((0, padded - offsets), (0, 0), (0, 0)))
    w_rows_t = w_rows.transpose(0, 2, 1)
    cotangent_full = lax.all_gather(cotangent[0], "chan", axis=1, tiled=True)

    rim_shape = shape((rim_count, half, width), BF16)
    block_shape = shape((tile_blocks, half, width), BF16)
    if merged:
        near = to_rows([merge] * tile_rows, tile_rows)
        log_blocks = pl.pallas_call(
            copy_kernel,
            out_shape=shape(log_blocks.shape, BF16),
            in_specs=[VMEM],
            out_specs=VMEM,
            compiler_params=PARAMS,
        )(log_blocks)
        stacked, log_blocks = lax.optimization_barrier((jnp.stack(near), log_blocks))
        far = across(stacked)
        held_blocks = (tile_rows // 2 * tile_blocks, half, width)
        def far_sums(rows_away):
            return across(
                pl.pallas_call(
                    functools.partial(far_kernel, rows_away, depths, tile_blocks),
                    out_shape=shape(held_blocks, BF16),
                    in_specs=[SMEM] * 2 + [VMEM],
                    out_specs=VMEM,
                    compiler_params=PARAMS,
                )(send, far, log_blocks)
            )

        far_high = far_sums(range(tile_rows // 2, tile_rows))
        far_low = far_sums(range(tile_rows // 2))
        near_low, near_high, place = pl.pallas_call(
            functools.partial(near_kernel, tile_rows, depths, tile_blocks),
            out_shape=(shape(held_blocks, F32),) * 2 + (shape((log_count + 1,), jnp.int32),),
            in_specs=[SMEM] * (2 + tile_rows) + [VMEM],
            out_specs=(VMEM,) * 2 + (SMEM,),
            compiler_params=PARAMS,
        )(send, *near, far, log_blocks)
        add = functools.partial(
            pl.pallas_call,
            add_kernel,
            in_specs=[VMEM] * 2,
            out_specs=(VMEM,) * 2,
            compiler_params=PARAMS,
        )
        high = add(out_shape=(block_shape,) * 2)(near_high, far_high)
        low = add(out_shape=(shape((tile_blocks, half, width), F32), block_shape))(
            near_low, far_low
        )
        incoming = to_rows([*low, *high], tile_rows)
    else:
        pick_table = (
            send.reshape(-1)[:, None] == jnp.arange(log_count, dtype=jnp.int32)[None, :]
        ).astype(BF16)
        outgoing = jnp.dot(
            pick_table, log_blocks.reshape(log_count, half * width), preferred_element_type=F32
        ).astype(BF16)
        incoming = relay(outgoing.reshape(tile_count, capacity, half, width))
        place_table = (
            jnp.arange(tile_blocks, dtype=jnp.int32)[:, None] == merge.reshape(-1)[None, :]
        ).astype(BF16)
        incoming = jnp.dot(
            place_table,
            incoming.reshape(tile_count * capacity, half * width),
            preferred_element_type=F32,
        )
        incoming = [incoming.astype(BF16).reshape(tile_blocks, half, width)]
    features, *sends = pl.pallas_call(
        functools.partial(merge_kernel, swaps),
        out_shape=(block_shape,) + (rim_shape,) * len(swaps),
        in_specs=[SMEM] + [VMEM] * len(incoming),
        out_specs=(VMEM,) * (1 + len(swaps)),
        compiler_params=PARAMS,
    )(halo, *incoming)
    received = swap_all(swaps, sends)

    pairs_total = padded * pair_slots
    part, columns = pl.pallas_call(
        functools.partial(forward_kernel, len(swaps), chunk),
        out_shape=(shape((channels, own_total), F32), shape((half, pairs_total), BF16)),
        in_specs=[VMEM] * (4 + len(swaps)),
        out_specs=(VMEM, VMEM),
        scratch_shapes=[
            pltpu.VMEM((2 * channels, pairs_total), BF16),
            pltpu.VMEM((span, pairs_total), BF16),
        ],
        compiler_params=PARAMS,
    )(features, *received, source_rows, target_rows, w_rows_t)
    other = lax.ppermute(part, "chan", [(0, 1), (1, 0)])

    grad_columns, own_grad, *rims = pl.pallas_call(
        functools.partial(input_grad_kernel, chunk),
        out_shape=(
            shape((channels, pairs_total), BF16),
            shape((tile_blocks, half, width), F32),
        )
        + (rim_shape,) * len(swaps),
        in_specs=[VMEM] * 6,
        out_specs=(VMEM,) * (2 + len(swaps)),
        scratch_shapes=[
            pltpu.VMEM((held_total // 2 * half, pairs_total), BF16),
            pltpu.VMEM((span, pairs_total), BF16),
        ],
        compiler_params=PARAMS,
    )(part, other, cotangent_full, source_rows, target_rows, w_rows)
    returned = swap_all(swaps, rims)
    portions = depths if merged else 1
    portion = (padded // portions * half, channels)
    activations, keep, *cross = pl.pallas_call(
        weight_grad_kernel,
        out_shape=(block_shape, shape(portion, F32)) + (shape(portion, BF16),) * (portions - 1),
        in_specs=[VMEM] * 4,
        out_specs=(VMEM,) * (1 + portions),
        scratch_shapes=[pltpu.VMEM((portions, *portion), F32)],
        compiler_params=PARAMS,
    )(part, other, columns, grad_columns)
    scale = float(tile_count * pair_slots) ** (-0.5)
    if merged:
        cross, returned = lax.optimization_barrier((cross, returned))
    tile_grad = pl.pallas_call(
        functools.partial(tile_grad_kernel, swaps),
        out_shape=block_shape,
        in_specs=[SMEM] + [VMEM] * (1 + len(swaps)),
        out_specs=VMEM,
        scratch_shapes=[pltpu.VMEM((tile_blocks, half, width), F32)],
        compiler_params=PARAMS,
    )(halo, own_grad, *returned)

    if merged:
        rows = portion[0] // tile_rows
        row_terms = pl.pallas_call(
            row_sum_kernel,
            out_shape=(shape((rows, channels), F32),)
            + (shape((rows, channels), BF16),) * (tile_rows - 1),
            in_specs=[VMEM] * 2,
            out_specs=(VMEM,) * tile_rows,
            scratch_shapes=[pltpu.VMEM(portion, F32)],
            compiler_params=PARAMS,
        )(keep, across(cross[0]))
        column_rows = tile_rows * tile_blocks * half
        bulk, shard = pl.pallas_call(
            functools.partial(column_kernel, tile_rows),
            out_shape=(shape((column_rows + rows, channels), BF16), shape((rows, channels), BF16)),
            in_specs=[VMEM] * (2 * tile_rows),
            out_specs=(VMEM,) * 2,
            compiler_params=PARAMS,
        )(*to_rows([tile_grad] * tile_rows, tile_rows), *to_rows(row_terms, tile_rows))
        other_bulk = across(bulk)
        shards = to_rows([shard] * tile_rows, tile_rows)
        last, other_bulk = lax.optimization_barrier((jnp.concatenate(shards[1:]), other_bulk))
        grad_log = pl.pallas_call(
            spread_kernel,
            out_shape=shape((log_count, half, width), BF16),
            in_specs=[SMEM] + [VMEM] * 2,
            out_specs=VMEM,
            scratch_shapes=[pltpu.VMEM((2 * column_rows, width), BF16)],
            compiler_params=PARAMS,
        )(place, bulk, other_bulk)
        grad_weight = pl.pallas_call(
            functools.partial(weight_kernel, scale, tile_rows),
            out_shape=shape((offsets * half, channels), F32),
            in_specs=[VMEM] * (tile_rows + 2),
            out_specs=VMEM,
            scratch_shapes=[pltpu.VMEM((padded * half, channels), F32)],
            compiler_params=PARAMS,
        )(*shards, other_bulk, across(last))
    else:
        back_blocks = jnp.dot(
            place_table.T,
            tile_grad.reshape(tile_blocks, half * width),
            preferred_element_type=F32,
        ).astype(BF16)
        back = relay(back_blocks.reshape(tile_count, capacity, half, width))
        grad_log = jnp.dot(
            pick_table.T,
            back.reshape(tile_count * capacity, half * width),
            preferred_element_type=F32,
        ).astype(BF16)
        grad_weight = lax.psum(keep[: offsets * half], TILES_AXES) * scale
    return (
        activations[None],
        grad_log.reshape(1, log_count, half, width),
        grad_weight.reshape(offsets, half, channels),
    )


def solution(mesh):
    split = ("groups", "tile", "depth")
    in_specs = (
        P(split, None, "chan", None),
        P(split, None, None),
        P(split, None, None),
        P(split, None, None),
        P(split, None, None),
        P(split, None, None),
        P(split, None),
        P(),
        P(split, None, "chan", None),
    )
    out_specs = (
        P(split, None, "chan", None),
        P(split, None, "chan", None),
        P("groups", "chan", None),
    )
    return jax.shard_map(local, mesh=mesh, in_specs=in_specs, out_specs=out_specs, check_vma=False)
```

```python
import functools

import jax
import jax.numpy as jnp
from jax import lax
from jax.experimental import pallas as pl
from jax.experimental.pallas import tpu as pltpu
from jax.sharding import PartitionSpec as P

F32 = jnp.float32
BF16 = jnp.bfloat16
TILES_AXES = ("tile", "depth")
VMEM = pl.BlockSpec(memory_space=pltpu.VMEM)
SMEM = pl.BlockSpec(memory_space=pltpu.SMEM)
PARAMS = pltpu.CompilerParams(vmem_limit_bytes=24 * 1024 * 1024)


def shape(dims, dtype):
    return jax.ShapeDtypeStruct(dims, dtype)


def pair_lists(size):
    return [
        [pair for i in range(first, size - 1, 2) for pair in ((i, i + 1), (i + 1, i))]
        for first in (0, 1)
    ]


def exchanges(tile_rows, depths):
    found = []
    for axis, size in (("tile", tile_rows), ("depth", depths)):
        for parity, pairs in enumerate(pair_lists(size)):
            if pairs:
                found.append((axis, parity, pairs))
    return found


def direction(axis, parity):
    place = lax.axis_index(axis) % 2
    upper = (place == parity).astype(jnp.int32)
    return upper + (0 if axis == "tile" else 2)


def xor_pairs(size, distance):
    return [(i, i ^ distance) for i in range(size)]


def merge_column(jx, rows_away, depths, tile_blocks, send_ref, tables, log_ref, emit):
    i, j = lax.axis_index("tile"), lax.axis_index("depth")
    me = i * depths + j
    half, width = log_ref.shape[1:]
    for d in rows_away:
        p = (i ^ d) * depths + (j ^ jx)
        totals = [jnp.zeros((half, width), F32) for _ in range(tile_blocks)]
        for c in range(send_ref.shape[1]):
            block = send_ref[p, c]
            wanted = jnp.where(block >= 0, tables(d, me, c), -1)
            rows = log_ref[jnp.maximum(block, 0)].astype(F32)
            for m in range(tile_blocks):
                totals[m] = totals[m] + rows * jnp.where(wanted == m, 1.0, 0.0)
        for m in range(tile_blocks):
            emit(d, m, totals[m])


def copy_kernel(in_ref, out_ref):
    out_ref[...] = in_ref[...]


def far_kernel(rows_away, depths, tile_blocks, send_ref, far_ref, log_ref, out_ref):
    def emit(d, m, total):
        out_ref[(d - rows_away[0]) * tile_blocks + m] = total.astype(BF16)

    merge_column(
        1, rows_away, depths, tile_blocks, send_ref, lambda *at: far_ref[at], log_ref, emit
    )


def near_kernel(tile_rows, depths, tile_blocks, *refs):
    send_ref, tables, log_ref, outs = refs[0], refs[1:-3], refs[-3], refs[-2:]
    per = tile_rows // len(outs)

    def emit(d, m, total):
        outs[d // per][(d % per) * tile_blocks + m] = total

    merge_column(
        0,
        range(tile_rows),
        depths,
        tile_blocks,
        send_ref,
        lambda d, *at: tables[d][at],
        log_ref,
        emit,
    )


def place_kernel(tile_rows, depths, tile_blocks, *refs):
    send_ref, tables, far_ref, place_ref = refs[0], refs[1:-2], refs[-2], refs[-1]
    i, j = lax.axis_index("tile"), lax.axis_index("depth")
    me = i * depths + j
    for jx in range(depths):
        for d in range(tile_rows):
            p = (i ^ d) * depths + (j ^ jx)
            for c in range(send_ref.shape[1]):
                block = send_ref[p, c]
                target = far_ref[d, me, c] if jx else tables[d][me, c]
                spot = jnp.where(block >= 0, block, place_ref.shape[0] - 1)
                place_ref[spot] = (jx * tile_rows + d) * tile_blocks + target


def add_kernel(near_ref, far_ref, *outs):
    count = near_ref.shape[0] // len(outs)
    for n, ref in enumerate(outs):
        for m in range(count):
            at = n * count + m
            ref[m] = (near_ref[at] + far_ref[at].astype(F32)).astype(ref.dtype)


def merge_kernel(swaps, halo_ref, *refs):
    incoming, features_ref = refs[: -1 - len(swaps)], refs[-1 - len(swaps)]
    sends = refs[-len(swaps) :] if swaps else ()
    for m in range(features_ref.shape[0]):
        total = incoming[0][m].astype(F32)
        for ref in incoming[1:]:
            total = total + ref[m].astype(F32)
        features_ref[m] = total.astype(BF16)
    pick_blocks(swaps, features_ref, halo_ref, sends)


def pick_blocks(swaps, features_ref, halo_ref, sends):
    for (axis, parity, _), send_ref in zip(swaps, sends):
        group = direction(axis, parity)
        for b in range(send_ref.shape[0]):
            send_ref[b] = features_ref[halo_ref[group, b]]


def table_row(ref, k):
    return ref[k : k + 1, :]


def one_hot(low, height):
    rows = lax.broadcasted_iota(jnp.int32, (height, low.shape[1]), 0).astype(F32).astype(BF16)
    low = low.astype(F32).astype(BF16)
    return jnp.where(rows == low, jnp.ones((), BF16), jnp.zeros((), BF16))


def pick_fold(fold, parts):
    picked = jnp.zeros_like(parts[0])
    for f, part in enumerate(parts):
        picked = jnp.where(fold == f, part, picked)
    return picked


def mask_fold(fold, f, part):
    return jnp.where(fold == f, part, jnp.zeros_like(part))


def gather_folds(folded, rows_ref, first_fold, chunk, half, base_of, emit):
    offsets, width = rows_ref.shape
    span = 2 * width
    for first in range(0, offsets, chunk):
        rows = [table_row(rows_ref, k) for k in range(first, first + chunk)]
        table = jnp.concatenate([one_hot(r & (span - 1), span) for r in rows], 1)
        gathered = jnp.dot(folded, table, preferred_element_type=F32).astype(BF16)
        for n, row in enumerate(rows):
            fold = (row // span).astype(F32).astype(BF16)
            picked = base_of(first + n)
            for f in range(folded.shape[0] // half):
                part = gathered[f * half : (f + 1) * half, n * width : (n + 1) * width]
                picked = jnp.where(fold == first_fold + f, part, picked)
            emit(first + n, picked)


def fold_blocks(blocks):
    return jnp.concatenate(
        [jnp.concatenate(blocks[n : n + 2], 1) for n in range(0, len(blocks), 2)], 0
    )


def own_columns_kernel(chunk, features_ref, source_ref, out_ref):
    count, half, width = features_ref.shape
    zero = jnp.zeros((half, width), BF16)

    def emit(k, picked):
        out_ref[:, k * width : (k + 1) * width] = picked

    folded = fold_blocks([features_ref[b] for b in range(count)])
    gather_folds(folded, source_ref, 0, chunk, half, lambda k: zero, emit)


def forward_kernel(own_folds, chunk, *refs):
    own_ref, source_ref, target_ref, weight_ref = refs[:4]
    received, (part_ref, columns_ref, values, places) = refs[4:-4], refs[-4:]
    channels, half = weight_ref.shape[1:]
    offsets, width = source_ref.shape
    span = 2 * width

    def lanes(k):
        return slice(k * width, (k + 1) * width)

    def emit(k, picked):
        columns_ref[:, lanes(k)] = picked
        product = jnp.dot(weight_ref[k], picked, preferred_element_type=F32).astype(BF16)
        target = table_row(target_ref, k)
        fold = (target // span).astype(F32).astype(BF16)
        places[:, lanes(k)] = one_hot(target & (span - 1), span)
        for f in range(2):
            values[f * channels : (f + 1) * channels, lanes(k)] = mask_fold(fold, f, product)

    blocks = [ref[b] for ref in received for b in range(ref.shape[0])]
    if blocks:
        gather_folds(
            fold_blocks(blocks),
            source_ref,
            own_folds,
            chunk,
            half,
            lambda k: own_ref[:, lanes(k)],
            emit,
        )
    else:
        for k in range(offsets):
            emit(k, own_ref[:, lanes(k)])
    total = lax.dot_general(
        values[...], places[...], (((1,), (1,)), ((), ())), preferred_element_type=F32
    )
    part_ref[:, :span] = total[:channels]
    part_ref[:, span:] = total[channels:]


def weight_grad_kernel(chunk, *refs):
    part_ref, other_ref, cotangent_ref, target_ref, columns_ref = refs[:5]
    act_ref, grad_columns_ref = refs[5:7]
    portions, held = refs[7:-1], refs[-1]
    tile_blocks, channels, width = cotangent_ref.shape
    half = columns_ref.shape[0]
    offsets = target_ref.shape[0]
    span = 2 * width
    portion = offsets // len(portions)
    here = lax.axis_index("depth") if len(portions) > 1 else 0
    preact = part_ref[...] + other_ref[...]
    gate = 1.0 / (1.0 + jnp.exp(-preact))
    cotangent = jnp.concatenate([cotangent_ref[b] for b in range(tile_blocks)], 1).astype(F32)
    grad = (cotangent * gate * (1.0 + preact * (1.0 - gate))).astype(BF16)
    folded = jnp.concatenate([grad[:, :span], grad[:, span:]], 0)
    for first in range(0, offsets, chunk):
        ks = range(first, first + chunk)
        rows = [table_row(target_ref, k) for k in ks]
        table = jnp.concatenate([one_hot(r & (span - 1), span) for r in rows], 1)
        gathered = jnp.dot(folded, table, preferred_element_type=F32).astype(BF16)
        for n, k in enumerate(ks):
            inside = slice(n * width, (n + 1) * width)
            lanes = slice(k * width, (k + 1) * width)
            fold = (rows[n] // span).astype(F32).astype(BF16)
            picked = pick_fold(fold, [gathered[:channels, inside], gathered[channels:, inside]])
            grad_columns_ref[:, lanes] = picked
            term = lax.dot_general(
                columns_ref[:, lanes],
                picked,
                (((1,), (1,)), ((), ())),
                preferred_element_type=F32,
            )
            row = (k % portion) * half
            held[(k // portion) ^ here, row : row + half, :] = term
    for n, ref in enumerate(portions):
        ref[...] = held[n].astype(ref.dtype)
    start = pl.multiple_of(lax.axis_index("chan") * half, half)
    own = part_ref[pl.ds(start, half), :] + other_ref[pl.ds(start, half), :]
    own = own / (1.0 + jnp.exp(-own))
    for b in range(tile_blocks):
        act_ref[b] = own[:, b * width : (b + 1) * width].astype(BF16)


def input_grad_kernel(grad_columns_ref, source_ref, weight_ref, own_ref, *refs):
    rims, (values, places) = refs[:-2], refs[-2:]
    tile_blocks = own_ref.shape[0]
    offsets, half, _ = weight_ref.shape
    width = source_ref.shape[1]
    span = 2 * width
    folds = values.shape[0] // half
    for k in range(offsets):
        lanes = slice(k * width, (k + 1) * width)
        returned = jnp.dot(
            weight_ref[k], grad_columns_ref[:, lanes], preferred_element_type=F32
        ).astype(BF16)
        source = table_row(source_ref, k)
        fold = (source // span).astype(F32).astype(BF16)
        places[:, lanes] = one_hot(source & (span - 1), span)
        for f in range(folds):
            values[f * half : (f + 1) * half, lanes] = mask_fold(fold, f, returned)
    total = lax.dot_general(
        values[...], places[...], (((1,), (1,)), ((), ())), preferred_element_type=F32
    )

    def block(b):
        return total[(b // 2) * half : (b // 2 + 1) * half, (b % 2) * width : (b % 2 + 1) * width]

    for b in range(tile_blocks):
        own_ref[b] = block(b)
    place = tile_blocks
    for rim in rims:
        for b in range(rim.shape[0]):
            rim[b] = block(place).astype(BF16)
            place += 1


def add_rims(swaps, halo_ref, total, received):
    for (axis, parity, _), ref in zip(swaps, received):
        group = direction(axis, parity)
        for b in range(ref.shape[0]):
            where = halo_ref[group, b]
            total[where] = total[where] + ref[b].astype(F32)


def tile_grad_kernel(swaps, halo_ref, own_ref, *refs):
    received, (out_ref, total) = refs[:-2], refs[-2:]
    total[...] = own_ref[...]
    add_rims(swaps, halo_ref, total, received)
    out_ref[...] = total[...].astype(BF16)


def collect_kernel(swaps, halo_ref, own_ref, keep_ref, crossed_ref, *refs):
    received, refs = refs[: len(swaps)], refs[len(swaps) :]
    (grad_ref, share_ref, *sends), (total, terms) = refs[:-2], refs[-2:]
    blocks, half, _ = own_ref.shape
    terms[...] = keep_ref[...] + crossed_ref[...].astype(F32)
    total[...] = own_ref[...]
    add_rims(swaps, halo_ref, total, received)
    for b in range(blocks):
        grad_ref[b * half : (b + 1) * half, :] = total[b].astype(BF16)
    i = lax.axis_index("tile")
    rows = share_ref.shape[0]
    for d, ref in enumerate((share_ref, *sends)):
        share = terms[pl.ds(pl.multiple_of((i ^ d) * rows, rows), rows), :]
        if d:
            ref[: blocks * half, :] = grad_ref[...]
            ref[blocks * half :, :] = share.astype(BF16)
        else:
            ref[...] = share


def column_kernel(grad_ref, share_ref, *refs):
    received, (bulk_ref, shard_ref) = refs[:-2], refs[-2:]
    rows = grad_ref.shape[0]
    bulk_ref[:rows, :] = grad_ref[...]
    total = share_ref[...]
    for d, ref in enumerate(received, 1):
        bulk_ref[d * rows : (d + 1) * rows, :] = ref[:rows, :]
        total = total + ref[rows:, :].astype(F32)
    shard_ref[...] = total.astype(BF16)
    bulk_ref[(len(received) + 1) * rows :, :] = shard_ref[...]


def spread_kernel(place_ref, own_ref, other_ref, out_ref, held):
    rows = held.shape[0] // 2
    height = out_ref.shape[1]
    held[:rows, :] = own_ref[:rows, :]
    held[rows:, :] = other_ref[:rows, :]
    for b in range(out_ref.shape[0]):
        first = pl.multiple_of(place_ref[b] * height, height)
        out_ref[b] = held[pl.ds(first, height), :]


def weight_kernel(scale, tile_rows, *refs):
    near, (bulk_ref, far_ref, out_ref, held) = refs[:tile_rows], refs[tile_rows:]
    i, j = lax.axis_index("tile"), lax.axis_index("depth")
    rows = near[0].shape[0]
    for jx in range(2):
        for d in range(tile_rows):
            if jx == 0:
                shard = near[d][...]
            elif d == 0:
                shard = bulk_ref[bulk_ref.shape[0] - rows :, :]
            else:
                shard = far_ref[(d - 1) * rows : d * rows, :]
            start = pl.multiple_of(((j ^ jx) * tile_rows + (i ^ d)) * rows, rows)
            held[pl.ds(start, rows), :] = shard.astype(F32) * scale
    out_ref[...] = held[: out_ref.shape[0], :]


def swap_all(swaps, arrays):
    return [
        lax.ppermute(array, axis, pairs) for (axis, _, pairs), array in zip(swaps, arrays)
    ]


def to_rows(arrays, tile_rows):
    return [arrays[0]] + [
        lax.ppermute(arrays[d], "tile", xor_pairs(tile_rows, d)) for d in range(1, tile_rows)
    ]


def across(array):
    return lax.ppermute(array, "depth", [(0, 1), (1, 0)])


def relay(outgoing):
    return lax.all_to_all(outgoing, TILES_AXES, split_axis=0, concat_axis=0, tiled=True)


def local(
    log_features, send_slot, merge_slot, halo_list, in_rows, out_rows, pair_count, weight, cotangent
):
    tile_rows = lax.axis_size("tile")
    depths = lax.axis_size("depth")
    tile_count = tile_rows * depths
    log_blocks = log_features[0]
    log_count, half, width = log_blocks.shape
    tile_blocks = cotangent.shape[1]
    offsets, channels, _ = weight.shape
    capacity = send_slot.shape[2]
    rim_count = halo_list.shape[2]
    pair_slots = in_rows.shape[2]
    own_total = tile_blocks * width
    span = 2 * width
    chunk = 4
    padded = -(-offsets // chunk) * chunk
    swaps = exchanges(tile_rows, depths)
    merged = (tile_rows, depths) == (4, 2) and capacity >= tile_blocks
    send, merge, halo = send_slot[0], merge_slot[0], halo_list[0]

    block_of = in_rows[0] // width
    group_of = (block_of - tile_blocks) // rim_count
    held_total = tile_blocks + len(swaps) * rim_count
    new_block = jnp.where(block_of < tile_blocks, block_of, held_total)
    for place, (axis, parity, _) in enumerate(swaps):
        hit = (block_of >= tile_blocks) & (group_of == direction(axis, parity))
        inside = (block_of - tile_blocks) % rim_count
        new_block = jnp.where(hit, tile_blocks + place * rim_count + inside, new_block)
    live = jnp.arange(pair_slots, dtype=jnp.int32)[None, :] < pair_count[0][:, None]
    source_rows = jnp.where(live, new_block * width + in_rows[0] % width, held_total * width)
    target_rows = jnp.where(live, out_rows[0], own_total)
    extra = ((0, padded - offsets), (0, 0))
    source_rows = jnp.pad(source_rows, extra, constant_values=held_total * width)
    target_rows = jnp.pad(target_rows, extra, constant_values=own_total)
    w_rows = lax.dynamic_slice_in_dim(weight, lax.axis_index("chan") * half, half, 1)
    w_rows = jnp.pad(w_rows, ((0, padded - offsets), (0, 0), (0, 0)))
    w_rows_t = w_rows.transpose(0, 2, 1)
    cotangent_full = lax.all_gather(cotangent[0], "chan", axis=1, tiled=True)

    rim_shape = shape((rim_count, half, width), BF16)
    block_shape = shape((tile_blocks, half, width), BF16)
    if merged:
        near = to_rows([merge] * tile_rows, tile_rows)
        log_blocks = pl.pallas_call(
            copy_kernel,
            out_shape=shape(log_blocks.shape, BF16),
            in_specs=[VMEM],
            out_specs=VMEM,
            compiler_params=PARAMS,
        )(log_blocks)
        stacked, log_blocks = lax.optimization_barrier((jnp.stack(near), log_blocks))
        far = across(stacked)
        held_blocks = (tile_rows // 2 * tile_blocks, half, width)
        def far_sums(rows_away):
            return across(
                pl.pallas_call(
                    functools.partial(far_kernel, rows_away, depths, tile_blocks),
                    out_shape=shape(held_blocks, BF16),
                    in_specs=[SMEM] * 2 + [VMEM],
                    out_specs=VMEM,
                    compiler_params=PARAMS,
                )(send, far, log_blocks)
            )

        far_high = far_sums(range(tile_rows // 2, tile_rows))
        far_low = far_sums(range(tile_rows // 2))
        near_low, near_high = pl.pallas_call(
            functools.partial(near_kernel, tile_rows, depths, tile_blocks),
            out_shape=(shape(held_blocks, F32),) * 2,
            in_specs=[SMEM] * (1 + tile_rows) + [VMEM],
            out_specs=(VMEM,) * 2,
            compiler_params=PARAMS,
        )(send, *near, log_blocks)
        place = pl.pallas_call(
            functools.partial(place_kernel, tile_rows, depths, tile_blocks),
            out_shape=shape((log_count + 1,), jnp.int32),
            in_specs=[SMEM] * (2 + tile_rows),
            out_specs=SMEM,
            compiler_params=PARAMS,
        )(send, *near, far)
        add = functools.partial(
            pl.pallas_call,
            add_kernel,
            in_specs=[VMEM] * 2,
            out_specs=(VMEM,) * 2,
            compiler_params=PARAMS,
        )
        high = add(out_shape=(block_shape,) * 2)(near_high, far_high)
        low = add(out_shape=(shape((tile_blocks, half, width), F32), block_shape))(
            near_low, far_low
        )
        incoming = to_rows([*low, *high], tile_rows)
        incoming, place = lax.optimization_barrier((incoming, place))
    else:
        pick_table = (
            send.reshape(-1)[:, None] == jnp.arange(log_count, dtype=jnp.int32)[None, :]
        ).astype(BF16)
        outgoing = jnp.dot(
            pick_table, log_blocks.reshape(log_count, half * width), preferred_element_type=F32
        ).astype(BF16)
        incoming = relay(outgoing.reshape(tile_count, capacity, half, width))
        place_table = (
            jnp.arange(tile_blocks, dtype=jnp.int32)[:, None] == merge.reshape(-1)[None, :]
        ).astype(BF16)
        incoming = jnp.dot(
            place_table,
            incoming.reshape(tile_count * capacity, half * width),
            preferred_element_type=F32,
        )
        incoming = [incoming.astype(BF16).reshape(tile_blocks, half, width)]
    features, *sends = pl.pallas_call(
        functools.partial(merge_kernel, swaps),
        out_shape=(block_shape,) + (rim_shape,) * len(swaps),
        in_specs=[SMEM] + [VMEM] * len(incoming),
        out_specs=(VMEM,) * (1 + len(swaps)),
        compiler_params=PARAMS,
    )(halo, *incoming)
    received = swap_all(swaps, sends)

    pairs_total = padded * pair_slots
    own_columns = pl.pallas_call(
        functools.partial(own_columns_kernel, chunk),
        out_shape=shape((half, pairs_total), BF16),
        in_specs=[VMEM] * 2,
        out_specs=VMEM,
        compiler_params=PARAMS,
    )(features, source_rows)
    part, columns = pl.pallas_call(
        functools.partial(forward_kernel, tile_blocks // 2, chunk),
        out_shape=(shape((channels, own_total), F32), shape((half, pairs_total), BF16)),
        in_specs=[VMEM] * (4 + len(swaps)),
        out_specs=(VMEM, VMEM),
        scratch_shapes=[
            pltpu.VMEM((2 * channels, pairs_total), BF16),
            pltpu.VMEM((span, pairs_total), BF16),
        ],
        compiler_params=PARAMS,
    )(own_columns, source_rows, target_rows, w_rows_t, *received)
    other = lax.ppermute(part, "chan", [(0, 1), (1, 0)])

    portions = depths if merged else 1
    portion = (padded // portions * half, channels)
    activations, grad_columns, keep, *cross = pl.pallas_call(
        functools.partial(weight_grad_kernel, chunk),
        out_shape=(block_shape, shape((channels, pairs_total), BF16), shape(portion, F32))
        + (shape(portion, BF16),) * (portions - 1),
        in_specs=[VMEM] * 5,
        out_specs=(VMEM,) * (2 + portions),
        scratch_shapes=[pltpu.VMEM((portions, *portion), F32)],
        compiler_params=PARAMS,
    )(part, other, cotangent_full, target_rows, columns)
    scale = float(tile_count * pair_slots) ** (-0.5)
    own_grad, *rims = pl.pallas_call(
        input_grad_kernel,
        out_shape=(shape((tile_blocks, half, width), F32),) + (rim_shape,) * len(swaps),
        in_specs=[VMEM] * 3,
        out_specs=(VMEM,) * (1 + len(swaps)),
        scratch_shapes=[
            pltpu.VMEM((held_total // 2 * half, pairs_total), BF16),
            pltpu.VMEM((span, pairs_total), BF16),
        ],
        compiler_params=PARAMS,
    )(grad_columns, source_rows, w_rows)
    returned = swap_all(swaps, rims)
    if merged:
        rows = portion[0] // tile_rows
        own_rows = tile_blocks * half
        column_rows = tile_rows * own_rows
        grad, share, *sends = pl.pallas_call(
            functools.partial(collect_kernel, swaps),
            out_shape=(shape((own_rows, width), BF16), shape((rows, channels), F32))
            + (shape((own_rows + rows, width), BF16),) * (tile_rows - 1),
            in_specs=[SMEM] + [VMEM] * (3 + len(swaps)),
            out_specs=(VMEM,) * (1 + tile_rows),
            scratch_shapes=[
                pltpu.VMEM((tile_blocks, half, width), F32),
                pltpu.VMEM(portion, F32),
            ],
            compiler_params=PARAMS,
        )(halo, own_grad, keep, across(cross[0]), *returned)
        bulk, shard = pl.pallas_call(
            column_kernel,
            out_shape=(shape((column_rows + rows, channels), BF16), shape((rows, channels), BF16)),
            in_specs=[VMEM] * (1 + tile_rows),
            out_specs=(VMEM,) * 2,
            compiler_params=PARAMS,
        )(grad, *to_rows([share, *sends], tile_rows))
        other_bulk = across(bulk)
        shards = to_rows([shard] * tile_rows, tile_rows)
        last, other_bulk = lax.optimization_barrier((jnp.concatenate(shards[1:]), other_bulk))
        grad_log = pl.pallas_call(
            spread_kernel,
            out_shape=shape((log_count, half, width), BF16),
            in_specs=[SMEM] + [VMEM] * 2,
            out_specs=VMEM,
            scratch_shapes=[pltpu.VMEM((2 * column_rows, width), BF16)],
            compiler_params=PARAMS,
        )(place, bulk, other_bulk)
        grad_weight = pl.pallas_call(
            functools.partial(weight_kernel, scale, tile_rows),
            out_shape=shape((offsets * half, channels), F32),
            in_specs=[VMEM] * (tile_rows + 2),
            out_specs=VMEM,
            scratch_shapes=[pltpu.VMEM((padded * half, channels), F32)],
            compiler_params=PARAMS,
        )(*shards, other_bulk, across(last))
    else:
        tile_grad = pl.pallas_call(
            functools.partial(tile_grad_kernel, swaps),
            out_shape=block_shape,
            in_specs=[SMEM] + [VMEM] * (1 + len(swaps)),
            out_specs=VMEM,
            scratch_shapes=[pltpu.VMEM((tile_blocks, half, width), F32)],
            compiler_params=PARAMS,
        )(halo, own_grad, *returned)
        back_blocks = jnp.dot(
            place_table.T,
            tile_grad.reshape(tile_blocks, half * width),
            preferred_element_type=F32,
        ).astype(BF16)
        back = relay(back_blocks.reshape(tile_count, capacity, half, width))
        grad_log = jnp.dot(
            pick_table.T,
            back.reshape(tile_count * capacity, half * width),
            preferred_element_type=F32,
        ).astype(BF16)
        grad_weight = lax.psum(keep[: offsets * half], TILES_AXES) * scale
    return (
        activations[None],
        grad_log.reshape(1, log_count, half, width),
        grad_weight.reshape(offsets, half, channels),
    )


def solution(mesh):
    split = ("groups", "tile", "depth")
    in_specs = (
        P(split, None, "chan", None),
        P(split, None, None),
        P(split, None, None),
        P(split, None, None),
        P(split, None, None),
        P(split, None, None),
        P(split, None),
        P(),
        P(split, None, "chan", None),
    )
    out_specs = (
        P(split, None, "chan", None),
        P(split, None, "chan", None),
        P("groups", "chan", None),
    )
    return jax.shard_map(local, mesh=mesh, in_specs=in_specs, out_specs=out_specs, check_vma=False)
```

```python
import functools

import jax
import jax.numpy as jnp
from jax import lax
from jax.experimental import pallas as pl
from jax.experimental.pallas import tpu as pltpu
from jax.sharding import PartitionSpec as P

F32 = jnp.float32
BF16 = jnp.bfloat16
TILES_AXES = ("tile", "depth")
VMEM = pl.BlockSpec(memory_space=pltpu.VMEM)
SMEM = pl.BlockSpec(memory_space=pltpu.SMEM)
PARAMS = pltpu.CompilerParams(vmem_limit_bytes=24 * 1024 * 1024)


def shape(dims, dtype):
    return jax.ShapeDtypeStruct(dims, dtype)


def pair_lists(size):
    return [
        [pair for i in range(first, size - 1, 2) for pair in ((i, i + 1), (i + 1, i))]
        for first in (0, 1)
    ]


def exchanges(tile_rows, depths):
    found = []
    for axis, size in (("tile", tile_rows), ("depth", depths)):
        for parity, pairs in enumerate(pair_lists(size)):
            if pairs:
                found.append((axis, parity, pairs))
    return found


def direction(axis, parity):
    place = lax.axis_index(axis) % 2
    upper = (place == parity).astype(jnp.int32)
    return upper + (0 if axis == "tile" else 2)


def xor_pairs(size, distance):
    return [(i, i ^ distance) for i in range(size)]


def merge_column(jx, rows_away, depths, tile_blocks, send_ref, tables, log_ref, emit):
    i, j = lax.axis_index("tile"), lax.axis_index("depth")
    me = i * depths + j
    half, width = log_ref.shape[1:]
    for d in rows_away:
        p = (i ^ d) * depths + (j ^ jx)
        totals = [jnp.zeros((half, width), F32) for _ in range(tile_blocks)]
        for c in range(send_ref.shape[1]):
            block = send_ref[p, c]
            wanted = jnp.where(block >= 0, tables(d, me, c), -1)
            rows = log_ref[jnp.maximum(block, 0)].astype(F32)
            for m in range(tile_blocks):
                totals[m] = totals[m] + rows * jnp.where(wanted == m, 1.0, 0.0)
        for m in range(tile_blocks):
            emit(d, m, totals[m])


def copy_kernel(in_ref, out_ref):
    out_ref[...] = in_ref[...]


def far_kernel(rows_away, depths, tile_blocks, send_ref, far_ref, log_ref, out_ref):
    def emit(d, m, total):
        out_ref[(d - rows_away[0]) * tile_blocks + m] = total.astype(BF16)

    merge_column(
        1, rows_away, depths, tile_blocks, send_ref, lambda *at: far_ref[at], log_ref, emit
    )


def near_kernel(tile_rows, depths, tile_blocks, *refs):
    send_ref, tables, log_ref, outs = refs[0], refs[1:-3], refs[-3], refs[-2:]
    per = tile_rows // len(outs)

    def emit(d, m, total):
        outs[d // per][(d % per) * tile_blocks + m] = total

    merge_column(
        0,
        range(tile_rows),
        depths,
        tile_blocks,
        send_ref,
        lambda d, *at: tables[d][at],
        log_ref,
        emit,
    )


def place_kernel(tile_rows, depths, tile_blocks, *refs):
    send_ref, tables, far_ref, place_ref = refs[0], refs[1:-2], refs[-2], refs[-1]
    i, j = lax.axis_index("tile"), lax.axis_index("depth")
    me = i * depths + j
    for jx in range(depths):
        for d in range(tile_rows):
            p = (i ^ d) * depths + (j ^ jx)
            for c in range(send_ref.shape[1]):
                block = send_ref[p, c]
                target = far_ref[d, me, c] if jx else tables[d][me, c]
                spot = jnp.where(block >= 0, block, place_ref.shape[0] - 1)
                place_ref[spot] = (jx * tile_rows + d) * tile_blocks + target


def add_kernel(near_ref, far_ref, *outs):
    count = near_ref.shape[0] // len(outs)
    for n, ref in enumerate(outs):
        for m in range(count):
            at = n * count + m
            ref[m] = (near_ref[at] + far_ref[at].astype(F32)).astype(ref.dtype)


def merge_kernel(swaps, halo_ref, *refs):
    incoming, features_ref = refs[: -1 - len(swaps)], refs[-1 - len(swaps)]
    sends = refs[-len(swaps) :] if swaps else ()
    for m in range(features_ref.shape[0]):
        total = incoming[0][m].astype(F32)
        for ref in incoming[1:]:
            total = total + ref[m].astype(F32)
        features_ref[m] = total.astype(BF16)
    pick_blocks(swaps, features_ref, halo_ref, sends)


def pick_blocks(swaps, features_ref, halo_ref, sends):
    for (axis, parity, _), send_ref in zip(swaps, sends):
        group = direction(axis, parity)
        for b in range(send_ref.shape[0]):
            send_ref[b] = features_ref[halo_ref[group, b]]


def table_row(ref, k):
    return ref[k : k + 1, :]


def one_hot(low, height):
    rows = lax.broadcasted_iota(jnp.int32, (height, low.shape[1]), 0).astype(F32).astype(BF16)
    low = low.astype(F32).astype(BF16)
    return jnp.where(rows == low, jnp.ones((), BF16), jnp.zeros((), BF16))


def pick_fold(fold, parts):
    picked = jnp.zeros_like(parts[0])
    for f, part in enumerate(parts):
        picked = jnp.where(fold == f, part, picked)
    return picked


def mask_fold(fold, f, part):
    return jnp.where(fold == f, part, jnp.zeros_like(part))


def gather_folds(folded, rows_ref, first_fold, chunk, half, base_of, emit):
    offsets, width = rows_ref.shape
    span = 2 * width
    for first in range(0, offsets, chunk):
        rows = [table_row(rows_ref, k) for k in range(first, first + chunk)]
        table = jnp.concatenate([one_hot(r & (span - 1), span) for r in rows], 1)
        gathered = jnp.dot(folded, table, preferred_element_type=F32).astype(BF16)
        for n, row in enumerate(rows):
            fold = (row // span).astype(F32).astype(BF16)
            picked = base_of(first + n)
            for f in range(folded.shape[0] // half):
                part = gathered[f * half : (f + 1) * half, n * width : (n + 1) * width]
                picked = jnp.where(fold == first_fold + f, part, picked)
            emit(first + n, picked)


def fold_blocks(blocks):
    return jnp.concatenate(
        [jnp.concatenate(blocks[n : n + 2], 1) for n in range(0, len(blocks), 2)], 0
    )


def own_columns_kernel(chunk, features_ref, source_ref, out_ref):
    count, half, width = features_ref.shape
    zero = jnp.zeros((half, width), BF16)

    def emit(k, picked):
        out_ref[:, k * width : (k + 1) * width] = picked

    folded = fold_blocks([features_ref[b] for b in range(count)])
    gather_folds(folded, source_ref, 0, chunk, half, lambda k: zero, emit)


def forward_kernel(own_folds, chunk, *refs):
    own_ref, source_ref, target_ref, weight_ref = refs[:4]
    received, (part_ref, columns_ref, values, places) = refs[4:-4], refs[-4:]
    channels, half = weight_ref.shape[1:]
    offsets, width = source_ref.shape
    span = 2 * width

    def lanes(k):
        return slice(k * width, (k + 1) * width)

    def emit(k, picked):
        columns_ref[:, lanes(k)] = picked
        product = jnp.dot(weight_ref[k], picked, preferred_element_type=F32).astype(BF16)
        target = table_row(target_ref, k)
        fold = (target // span).astype(F32).astype(BF16)
        places[:, lanes(k)] = one_hot(target & (span - 1), span)
        for f in range(2):
            values[f * channels : (f + 1) * channels, lanes(k)] = mask_fold(fold, f, product)

    blocks = [ref[b] for ref in received for b in range(ref.shape[0])]
    if blocks:
        gather_folds(
            fold_blocks(blocks),
            source_ref,
            own_folds,
            chunk,
            half,
            lambda k: own_ref[:, lanes(k)],
            emit,
        )
    else:
        for k in range(offsets):
            emit(k, own_ref[:, lanes(k)])
    total = lax.dot_general(
        values[...], places[...], (((1,), (1,)), ((), ())), preferred_element_type=F32
    )
    part_ref[:, :span] = total[:channels]
    part_ref[:, span:] = total[channels:]


def weight_grad_kernel(chunk, *refs):
    part_ref, other_ref, cotangent_ref, target_ref, columns_ref = refs[:5]
    act_ref, grad_columns_ref = refs[5:7]
    portions, held = refs[7:-1], refs[-1]
    tile_blocks, channels, width = cotangent_ref.shape
    half = columns_ref.shape[0]
    offsets = target_ref.shape[0]
    span = 2 * width
    portion = offsets // len(portions)
    here = lax.axis_index("depth") if len(portions) > 1 else 0
    preact = part_ref[...] + other_ref[...]
    gate = 1.0 / (1.0 + jnp.exp(-preact))
    cotangent = jnp.concatenate([cotangent_ref[b] for b in range(tile_blocks)], 1).astype(F32)
    grad = (cotangent * gate * (1.0 + preact * (1.0 - gate))).astype(BF16)
    folded = jnp.concatenate([grad[:, :span], grad[:, span:]], 0)
    for first in range(0, offsets, chunk):
        ks = range(first, first + chunk)
        rows = [table_row(target_ref, k) for k in ks]
        table = jnp.concatenate([one_hot(r & (span - 1), span) for r in rows], 1)
        gathered = jnp.dot(folded, table, preferred_element_type=F32).astype(BF16)
        for n, k in enumerate(ks):
            inside = slice(n * width, (n + 1) * width)
            lanes = slice(k * width, (k + 1) * width)
            fold = (rows[n] // span).astype(F32).astype(BF16)
            picked = pick_fold(fold, [gathered[:channels, inside], gathered[channels:, inside]])
            grad_columns_ref[:, lanes] = picked
            term = lax.dot_general(
                columns_ref[:, lanes],
                picked,
                (((1,), (1,)), ((), ())),
                preferred_element_type=F32,
            )
            row = (k % portion) * half
            held[(k // portion) ^ here, row : row + half, :] = term
    for n, ref in enumerate(portions):
        ref[...] = held[n].astype(ref.dtype)
    start = pl.multiple_of(lax.axis_index("chan") * half, half)
    own = part_ref[pl.ds(start, half), :] + other_ref[pl.ds(start, half), :]
    own = own / (1.0 + jnp.exp(-own))
    for b in range(tile_blocks):
        act_ref[b] = own[:, b * width : (b + 1) * width].astype(BF16)


def input_grad_kernel(grad_columns_ref, source_ref, weight_ref, own_ref, *refs):
    rims, (values, places) = refs[:-2], refs[-2:]
    tile_blocks = own_ref.shape[0]
    offsets, half, _ = weight_ref.shape
    width = source_ref.shape[1]
    span = 2 * width
    folds = values.shape[0] // half
    for k in range(offsets):
        lanes = slice(k * width, (k + 1) * width)
        returned = jnp.dot(
            weight_ref[k], grad_columns_ref[:, lanes], preferred_element_type=F32
        ).astype(BF16)
        source = table_row(source_ref, k)
        fold = (source // span).astype(F32).astype(BF16)
        places[:, lanes] = one_hot(source & (span - 1), span)
        for f in range(folds):
            values[f * half : (f + 1) * half, lanes] = mask_fold(fold, f, returned)
    total = lax.dot_general(
        values[...], places[...], (((1,), (1,)), ((), ())), preferred_element_type=F32
    )

    def block(b):
        return total[(b // 2) * half : (b // 2 + 1) * half, (b % 2) * width : (b % 2 + 1) * width]

    for b in range(tile_blocks):
        own_ref[b] = block(b)
    place = tile_blocks
    for rim in rims:
        for b in range(rim.shape[0]):
            rim[b] = block(place).astype(BF16)
            place += 1


def add_rims(swaps, halo_ref, total, received):
    for (axis, parity, _), ref in zip(swaps, received):
        group = direction(axis, parity)
        for b in range(ref.shape[0]):
            where = halo_ref[group, b]
            total[where] = total[where] + ref[b].astype(F32)


def tile_grad_kernel(swaps, halo_ref, own_ref, *refs):
    received, (out_ref, total) = refs[:-2], refs[-2:]
    total[...] = own_ref[...]
    add_rims(swaps, halo_ref, total, received)
    out_ref[...] = total[...].astype(BF16)


def collect_kernel(swaps, halo_ref, own_ref, keep_ref, crossed_ref, *refs):
    received, refs = refs[: len(swaps)], refs[len(swaps) :]
    (grad_ref, share_ref, *sends), (total, terms) = refs[:-2], refs[-2:]
    blocks, half, _ = own_ref.shape
    terms[...] = keep_ref[...] + crossed_ref[...].astype(F32)
    total[...] = own_ref[...]
    add_rims(swaps, halo_ref, total, received)
    for b in range(blocks):
        grad_ref[b * half : (b + 1) * half, :] = total[b].astype(BF16)
    i = lax.axis_index("tile")
    rows = share_ref.shape[0]
    for d, ref in enumerate((share_ref, *sends)):
        share = terms[pl.ds(pl.multiple_of((i ^ d) * rows, rows), rows), :]
        if d:
            ref[: blocks * half, :] = grad_ref[...]
            ref[blocks * half :, :] = share.astype(BF16)
        else:
            ref[...] = share


def column_kernel(early, share_ref, *refs):
    received, (bulk_ref, shard_ref) = refs[:-2], refs[-2:]
    rows = received[0].shape[0] - share_ref.shape[0]
    total = share_ref[...]
    for d, ref in enumerate(received):
        total = total + ref[rows:, :].astype(F32)
        if d >= early:
            bulk_ref[(d - early) * rows : (d - early + 1) * rows, :] = ref[:rows, :]
    shard_ref[...] = total.astype(BF16)
    bulk_ref[(len(received) - early) * rows :, :] = shard_ref[...]


def spread_kernel(place_ref, *refs):
    parts, (out_ref, held) = refs[:-2], refs[-2:]
    height = out_ref.shape[1]
    rows = parts[0].shape[0]
    first = 0
    for n, ref in enumerate(parts):
        count = rows if n % 3 < 2 else held.shape[0] // 2 - 2 * rows
        held[first : first + count, :] = ref[:count, :]
        first += count
    for b in range(out_ref.shape[0]):
        start = pl.multiple_of(place_ref[b] * height, height)
        out_ref[b] = held[pl.ds(start, height), :]


def weight_kernel(scale, tile_rows, *refs):
    near, (bulk_ref, *far), (out_ref, held) = refs[:tile_rows], refs[tile_rows:-2], refs[-2:]
    i, j = lax.axis_index("tile"), lax.axis_index("depth")
    rows = near[0].shape[0]
    for jx in range(2):
        for d in range(tile_rows):
            if jx == 0:
                shard = near[d][...]
            elif d == 0:
                shard = bulk_ref[bulk_ref.shape[0] - rows :, :]
            else:
                shard = far[d - 1][...]
            start = pl.multiple_of(((j ^ jx) * tile_rows + (i ^ d)) * rows, rows)
            held[pl.ds(start, rows), :] = shard.astype(F32) * scale
    out_ref[...] = held[: out_ref.shape[0], :]


def swap_all(swaps, arrays):
    return [
        lax.ppermute(array, axis, pairs) for (axis, _, pairs), array in zip(swaps, arrays)
    ]


def to_rows(arrays, tile_rows):
    return [arrays[0]] + [
        lax.ppermute(arrays[d], "tile", xor_pairs(tile_rows, d)) for d in range(1, tile_rows)
    ]


def across(array):
    return lax.ppermute(array, "depth", [(0, 1), (1, 0)])


def relay(outgoing):
    return lax.all_to_all(outgoing, TILES_AXES, split_axis=0, concat_axis=0, tiled=True)


def local(
    log_features, send_slot, merge_slot, halo_list, in_rows, out_rows, pair_count, weight, cotangent
):
    tile_rows = lax.axis_size("tile")
    depths = lax.axis_size("depth")
    tile_count = tile_rows * depths
    log_blocks = log_features[0]
    log_count, half, width = log_blocks.shape
    tile_blocks = cotangent.shape[1]
    offsets, channels, _ = weight.shape
    capacity = send_slot.shape[2]
    rim_count = halo_list.shape[2]
    pair_slots = in_rows.shape[2]
    own_total = tile_blocks * width
    span = 2 * width
    chunk = 4
    padded = -(-offsets // chunk) * chunk
    swaps = exchanges(tile_rows, depths)
    merged = (tile_rows, depths) == (4, 2) and capacity >= tile_blocks
    send, merge, halo = send_slot[0], merge_slot[0], halo_list[0]

    block_of = in_rows[0] // width
    group_of = (block_of - tile_blocks) // rim_count
    held_total = tile_blocks + len(swaps) * rim_count
    new_block = jnp.where(block_of < tile_blocks, block_of, held_total)
    for place, (axis, parity, _) in enumerate(swaps):
        hit = (block_of >= tile_blocks) & (group_of == direction(axis, parity))
        inside = (block_of - tile_blocks) % rim_count
        new_block = jnp.where(hit, tile_blocks + place * rim_count + inside, new_block)
    live = jnp.arange(pair_slots, dtype=jnp.int32)[None, :] < pair_count[0][:, None]
    source_rows = jnp.where(live, new_block * width + in_rows[0] % width, held_total * width)
    target_rows = jnp.where(live, out_rows[0], own_total)
    extra = ((0, padded - offsets), (0, 0))
    source_rows = jnp.pad(source_rows, extra, constant_values=held_total * width)
    target_rows = jnp.pad(target_rows, extra, constant_values=own_total)
    w_rows = lax.dynamic_slice_in_dim(weight, lax.axis_index("chan") * half, half, 1)
    w_rows = jnp.pad(w_rows, ((0, padded - offsets), (0, 0), (0, 0)))
    w_rows_t = w_rows.transpose(0, 2, 1)
    cotangent_full = lax.all_gather(cotangent[0], "chan", axis=1, tiled=True)

    rim_shape = shape((rim_count, half, width), BF16)
    block_shape = shape((tile_blocks, half, width), BF16)
    if merged:
        near = to_rows([merge] * tile_rows, tile_rows)
        log_blocks = pl.pallas_call(
            copy_kernel,
            out_shape=shape(log_blocks.shape, BF16),
            in_specs=[VMEM],
            out_specs=VMEM,
            compiler_params=PARAMS,
        )(log_blocks)
        stacked, log_blocks = lax.optimization_barrier((jnp.stack(near), log_blocks))
        far = across(stacked)
        held_blocks = (tile_rows // 2 * tile_blocks, half, width)
        def far_sums(rows_away):
            return across(
                pl.pallas_call(
                    functools.partial(far_kernel, rows_away, depths, tile_blocks),
                    out_shape=shape(held_blocks, BF16),
                    in_specs=[SMEM] * 2 + [VMEM],
                    out_specs=VMEM,
                    compiler_params=PARAMS,
                )(send, far, log_blocks)
            )

        far_high = far_sums(range(tile_rows // 2, tile_rows))
        far_low = far_sums(range(tile_rows // 2))
        near_low, near_high = pl.pallas_call(
            functools.partial(near_kernel, tile_rows, depths, tile_blocks),
            out_shape=(shape(held_blocks, F32),) * 2,
            in_specs=[SMEM] * (1 + tile_rows) + [VMEM],
            out_specs=(VMEM,) * 2,
            compiler_params=PARAMS,
        )(send, *near, log_blocks)
        place = pl.pallas_call(
            functools.partial(place_kernel, tile_rows, depths, tile_blocks),
            out_shape=shape((log_count + 1,), jnp.int32),
            in_specs=[SMEM] * (2 + tile_rows),
            out_specs=SMEM,
            compiler_params=PARAMS,
        )(send, *near, far)
        add = functools.partial(
            pl.pallas_call,
            add_kernel,
            in_specs=[VMEM] * 2,
            out_specs=(VMEM,) * 2,
            compiler_params=PARAMS,
        )
        high = add(out_shape=(block_shape,) * 2)(near_high, far_high)
        low = add(out_shape=(shape((tile_blocks, half, width), F32), block_shape))(
            near_low, far_low
        )
        incoming = to_rows([*low, *high], tile_rows)
        incoming, place = lax.optimization_barrier((incoming, place))
    else:
        pick_table = (
            send.reshape(-1)[:, None] == jnp.arange(log_count, dtype=jnp.int32)[None, :]
        ).astype(BF16)
        outgoing = jnp.dot(
            pick_table, log_blocks.reshape(log_count, half * width), preferred_element_type=F32
        ).astype(BF16)
        incoming = relay(outgoing.reshape(tile_count, capacity, half, width))
        place_table = (
            jnp.arange(tile_blocks, dtype=jnp.int32)[:, None] == merge.reshape(-1)[None, :]
        ).astype(BF16)
        incoming = jnp.dot(
            place_table,
            incoming.reshape(tile_count * capacity, half * width),
            preferred_element_type=F32,
        )
        incoming = [incoming.astype(BF16).reshape(tile_blocks, half, width)]
    features, *sends = pl.pallas_call(
        functools.partial(merge_kernel, swaps),
        out_shape=(block_shape,) + (rim_shape,) * len(swaps),
        in_specs=[SMEM] + [VMEM] * len(incoming),
        out_specs=(VMEM,) * (1 + len(swaps)),
        compiler_params=PARAMS,
    )(halo, *incoming)
    received = swap_all(swaps, sends)

    pairs_total = padded * pair_slots
    own_columns = pl.pallas_call(
        functools.partial(own_columns_kernel, chunk),
        out_shape=shape((half, pairs_total), BF16),
        in_specs=[VMEM] * 2,
        out_specs=VMEM,
        compiler_params=PARAMS,
    )(features, source_rows)
    part, columns = pl.pallas_call(
        functools.partial(forward_kernel, tile_blocks // 2, chunk),
        out_shape=(shape((channels, own_total), F32), shape((half, pairs_total), BF16)),
        in_specs=[VMEM] * (4 + len(swaps)),
        out_specs=(VMEM, VMEM),
        scratch_shapes=[
            pltpu.VMEM((2 * channels, pairs_total), BF16),
            pltpu.VMEM((span, pairs_total), BF16),
        ],
        compiler_params=PARAMS,
    )(own_columns, source_rows, target_rows, w_rows_t, *received)
    other = lax.ppermute(part, "chan", [(0, 1), (1, 0)])

    portions = depths if merged else 1
    portion = (padded // portions * half, channels)
    activations, grad_columns, keep, *cross = pl.pallas_call(
        functools.partial(weight_grad_kernel, chunk),
        out_shape=(block_shape, shape((channels, pairs_total), BF16), shape(portion, F32))
        + (shape(portion, BF16),) * (portions - 1),
        in_specs=[VMEM] * 5,
        out_specs=(VMEM,) * (2 + portions),
        scratch_shapes=[pltpu.VMEM((portions, *portion), F32)],
        compiler_params=PARAMS,
    )(part, other, cotangent_full, target_rows, columns)
    scale = float(tile_count * pair_slots) ** (-0.5)
    own_grad, *rims = pl.pallas_call(
        input_grad_kernel,
        out_shape=(shape((tile_blocks, half, width), F32),) + (rim_shape,) * len(swaps),
        in_specs=[VMEM] * 3,
        out_specs=(VMEM,) * (1 + len(swaps)),
        scratch_shapes=[
            pltpu.VMEM((held_total // 2 * half, pairs_total), BF16),
            pltpu.VMEM((span, pairs_total), BF16),
        ],
        compiler_params=PARAMS,
    )(grad_columns, source_rows, w_rows)
    returned = swap_all(swaps, rims)
    if merged:
        rows = portion[0] // tile_rows
        own_rows = tile_blocks * half
        column_rows = tile_rows * own_rows
        grad, share, *sends = pl.pallas_call(
            functools.partial(collect_kernel, swaps),
            out_shape=(shape((own_rows, width), BF16), shape((rows, channels), F32))
            + (shape((own_rows + rows, width), BF16),) * (tile_rows - 1),
            in_specs=[SMEM] + [VMEM] * (3 + len(swaps)),
            out_specs=(VMEM,) * (1 + tile_rows),
            scratch_shapes=[
                pltpu.VMEM((tile_blocks, half, width), F32),
                pltpu.VMEM(portion, F32),
            ],
            compiler_params=PARAMS,
        )(halo, own_grad, keep, across(cross[0]), *returned)
        received = to_rows([share, *sends], tile_rows)
        early = [across(grad), across(received[1])]
        received, early = lax.optimization_barrier((received, early))
        bulk, shard = pl.pallas_call(
            functools.partial(column_kernel, 1),
            out_shape=(
                shape((column_rows - 2 * own_rows + rows, channels), BF16),
                shape((rows, channels), BF16),
            ),
            in_specs=[VMEM] * tile_rows,
            out_specs=(VMEM,) * 2,
            compiler_params=PARAMS,
        )(*received)
        other_bulk = across(bulk)
        shards = to_rows([shard] * tile_rows, tile_rows)
        grad_log = pl.pallas_call(
            spread_kernel,
            out_shape=shape((log_count, half, width), BF16),
            in_specs=[SMEM] + [VMEM] * 6,
            out_specs=VMEM,
            scratch_shapes=[pltpu.VMEM((2 * column_rows, width), BF16)],
            compiler_params=PARAMS,
        )(place, grad, received[1], bulk, *early, other_bulk)
        far_shards = [across(part) for part in shards[1:]]
        far_shards, grad_log = lax.optimization_barrier((far_shards, grad_log))
        grad_weight = pl.pallas_call(
            functools.partial(weight_kernel, scale, tile_rows),
            out_shape=shape((offsets * half, channels), F32),
            in_specs=[VMEM] * (2 * tile_rows),
            out_specs=VMEM,
            scratch_shapes=[pltpu.VMEM((padded * half, channels), F32)],
            compiler_params=PARAMS,
        )(*shards, other_bulk, *far_shards)
    else:
        tile_grad = pl.pallas_call(
            functools.partial(tile_grad_kernel, swaps),
            out_shape=block_shape,
            in_specs=[SMEM] + [VMEM] * (1 + len(swaps)),
            out_specs=VMEM,
            scratch_shapes=[pltpu.VMEM((tile_blocks, half, width), F32)],
            compiler_params=PARAMS,
        )(halo, own_grad, *returned)
        back_blocks = jnp.dot(
            place_table.T,
            tile_grad.reshape(tile_blocks, half * width),
            preferred_element_type=F32,
        ).astype(BF16)
        back = relay(back_blocks.reshape(tile_count, capacity, half, width))
        grad_log = jnp.dot(
            pick_table.T,
            back.reshape(tile_count * capacity, half * width),
            preferred_element_type=F32,
        ).astype(BF16)
        grad_weight = lax.psum(keep[: offsets * half], TILES_AXES) * scale
    return (
        activations[None],
        grad_log.reshape(1, log_count, half, width),
        grad_weight.reshape(offsets, half, channels),
    )


def solution(mesh):
    split = ("groups", "tile", "depth")
    in_specs = (
        P(split, None, "chan", None),
        P(split, None, None),
        P(split, None, None),
        P(split, None, None),
        P(split, None, None),
        P(split, None, None),
        P(split, None),
        P(),
        P(split, None, "chan", None),
    )
    out_specs = (
        P(split, None, "chan", None),
        P(split, None, "chan", None),
        P("groups", "chan", None),
    )
    return jax.shard_map(local, mesh=mesh, in_specs=in_specs, out_specs=out_specs, check_vma=False)
```

```python
import functools

import jax
import jax.numpy as jnp
from jax import lax
from jax.experimental import pallas as pl
from jax.experimental.pallas import tpu as pltpu
from jax.sharding import PartitionSpec as P

F32 = jnp.float32
BF16 = jnp.bfloat16
TILES_AXES = ("tile", "depth")
VMEM = pl.BlockSpec(memory_space=pltpu.VMEM)
SMEM = pl.BlockSpec(memory_space=pltpu.SMEM)
PARAMS = pltpu.CompilerParams(vmem_limit_bytes=24 * 1024 * 1024)


def shape(dims, dtype):
    return jax.ShapeDtypeStruct(dims, dtype)


def pair_lists(size):
    return [
        [pair for i in range(first, size - 1, 2) for pair in ((i, i + 1), (i + 1, i))]
        for first in (0, 1)
    ]


def exchanges(tile_rows, depths):
    found = []
    for axis, size in (("tile", tile_rows), ("depth", depths)):
        for parity, pairs in enumerate(pair_lists(size)):
            if pairs:
                found.append((axis, parity, pairs))
    return found


def direction(axis, parity):
    place = lax.axis_index(axis) % 2
    upper = (place == parity).astype(jnp.int32)
    return upper + (0 if axis == "tile" else 2)


def xor_pairs(size, distance):
    return [(i, i ^ distance) for i in range(size)]


def merge_column(jx, rows_away, depths, tile_blocks, send_ref, tables, log_ref, emit):
    i, j = lax.axis_index("tile"), lax.axis_index("depth")
    me = i * depths + j
    half, width = log_ref.shape[1:]
    for d in rows_away:
        p = (i ^ d) * depths + (j ^ jx)
        totals = [jnp.zeros((half, width), F32) for _ in range(tile_blocks)]
        for c in range(send_ref.shape[1]):
            block = send_ref[p, c]
            wanted = jnp.where(block >= 0, tables(d, me, c), -1)
            rows = log_ref[jnp.maximum(block, 0)].astype(F32)
            for m in range(tile_blocks):
                totals[m] = totals[m] + rows * jnp.where(wanted == m, 1.0, 0.0)
        for m in range(tile_blocks):
            emit(d, m, totals[m])


def copy_kernel(in_ref, out_ref):
    out_ref[...] = in_ref[...]


def far_kernel(rows_away, depths, tile_blocks, send_ref, far_ref, log_ref, out_ref):
    def emit(d, m, total):
        out_ref[(d - rows_away[0]) * tile_blocks + m] = total.astype(BF16)

    merge_column(
        1, rows_away, depths, tile_blocks, send_ref, lambda *at: far_ref[at], log_ref, emit
    )


def near_kernel(tile_rows, depths, tile_blocks, *refs):
    send_ref, tables, log_ref, outs = refs[0], refs[1:-3], refs[-3], refs[-2:]
    per = tile_rows // len(outs)

    def emit(d, m, total):
        outs[d // per][(d % per) * tile_blocks + m] = total

    merge_column(
        0,
        range(tile_rows),
        depths,
        tile_blocks,
        send_ref,
        lambda d, *at: tables[d][at],
        log_ref,
        emit,
    )


def place_kernel(tile_rows, depths, tile_blocks, *refs):
    send_ref, tables, far_ref, place_ref = refs[0], refs[1:-2], refs[-2], refs[-1]
    i, j = lax.axis_index("tile"), lax.axis_index("depth")
    me = i * depths + j
    for jx in range(depths):
        for d in range(tile_rows):
            p = (i ^ d) * depths + (j ^ jx)
            for c in range(send_ref.shape[1]):
                block = send_ref[p, c]
                target = far_ref[d, me, c] if jx else tables[d][me, c]
                spot = jnp.where(block >= 0, block, place_ref.shape[0] - 1)
                place_ref[spot] = (jx * tile_rows + d) * tile_blocks + target


def add_kernel(near_ref, far_ref, *outs):
    count = near_ref.shape[0] // len(outs)
    for n, ref in enumerate(outs):
        for m in range(count):
            at = n * count + m
            ref[m] = (near_ref[at] + far_ref[at].astype(F32)).astype(ref.dtype)


def merge_kernel(swaps, halo_ref, *refs):
    incoming, features_ref = refs[: -1 - len(swaps)], refs[-1 - len(swaps)]
    sends = refs[-len(swaps) :] if swaps else ()
    for m in range(features_ref.shape[0]):
        total = incoming[0][m].astype(F32)
        for ref in incoming[1:]:
            total = total + ref[m].astype(F32)
        features_ref[m] = total.astype(BF16)
    pick_blocks(swaps, features_ref, halo_ref, sends)


def pick_blocks(swaps, features_ref, halo_ref, sends):
    for (axis, parity, _), send_ref in zip(swaps, sends):
        group = direction(axis, parity)
        for b in range(send_ref.shape[0]):
            send_ref[b] = features_ref[halo_ref[group, b]]


def table_row(ref, k):
    return ref[k : k + 1, :]


def one_hot(low, height):
    rows = lax.broadcasted_iota(jnp.int32, (height, low.shape[1]), 0).astype(F32).astype(BF16)
    low = low.astype(F32).astype(BF16)
    return jnp.where(rows == low, jnp.ones((), BF16), jnp.zeros((), BF16))


def pick_fold(fold, parts):
    picked = jnp.zeros_like(parts[0])
    for f, part in enumerate(parts):
        picked = jnp.where(fold == f, part, picked)
    return picked


def mask_fold(fold, f, part):
    return jnp.where(fold == f, part, jnp.zeros_like(part))


def gather_folds(folded, rows_ref, first_fold, chunk, half, base_of, emit):
    offsets, width = rows_ref.shape
    span = 2 * width
    for first in range(0, offsets, chunk):
        rows = [table_row(rows_ref, k) for k in range(first, first + chunk)]
        table = jnp.concatenate([one_hot(r & (span - 1), span) for r in rows], 1)
        gathered = jnp.dot(folded, table, preferred_element_type=F32).astype(BF16)
        for n, row in enumerate(rows):
            fold = (row // span).astype(F32).astype(BF16)
            picked = base_of(first + n)
            for f in range(folded.shape[0] // half):
                part = gathered[f * half : (f + 1) * half, n * width : (n + 1) * width]
                picked = jnp.where(fold == first_fold + f, part, picked)
            emit(first + n, picked)


def fold_blocks(blocks):
    return jnp.concatenate(
        [jnp.concatenate(blocks[n : n + 2], 1) for n in range(0, len(blocks), 2)], 0
    )


def own_columns_kernel(chunk, features_ref, source_ref, out_ref):
    count, half, width = features_ref.shape
    zero = jnp.zeros((half, width), BF16)

    def emit(k, picked):
        out_ref[:, k * width : (k + 1) * width] = picked

    folded = fold_blocks([features_ref[b] for b in range(count)])
    gather_folds(folded, source_ref, 0, chunk, half, lambda k: zero, emit)


def forward_kernel(own_folds, chunk, *refs):
    own_ref, source_ref, target_ref, weight_ref = refs[:4]
    received, (part_ref, columns_ref, values, places) = refs[4:-4], refs[-4:]
    channels, half = weight_ref.shape[1:]
    offsets, width = source_ref.shape
    span = 2 * width

    def lanes(k):
        return slice(k * width, (k + 1) * width)

    def emit(k, picked):
        columns_ref[:, lanes(k)] = picked
        product = jnp.dot(weight_ref[k], picked, preferred_element_type=F32).astype(BF16)
        target = table_row(target_ref, k)
        fold = (target // span).astype(F32).astype(BF16)
        places[:, lanes(k)] = one_hot(target & (span - 1), span)
        for f in range(2):
            values[f * channels : (f + 1) * channels, lanes(k)] = mask_fold(fold, f, product)

    blocks = [ref[b] for ref in received for b in range(ref.shape[0])]
    if blocks:
        gather_folds(
            fold_blocks(blocks),
            source_ref,
            own_folds,
            chunk,
            half,
            lambda k: own_ref[:, lanes(k)],
            emit,
        )
    else:
        for k in range(offsets):
            emit(k, own_ref[:, lanes(k)])
    total = lax.dot_general(
        values[...], places[...], (((1,), (1,)), ((), ())), preferred_element_type=F32
    )
    part_ref[:, :span] = total[:channels]
    part_ref[:, span:] = total[channels:]


def weight_grad_kernel(chunk, *refs):
    part_ref, other_ref, cotangent_ref, target_ref, columns_ref = refs[:5]
    act_ref, grad_columns_ref = refs[5:7]
    portions, held = refs[7:-1], refs[-1]
    tile_blocks, channels, width = cotangent_ref.shape
    half = columns_ref.shape[0]
    offsets = target_ref.shape[0]
    span = 2 * width
    portion = offsets // len(portions)
    here = lax.axis_index("depth") if len(portions) > 1 else 0
    preact = part_ref[...] + other_ref[...]
    gate = 1.0 / (1.0 + jnp.exp(-preact))
    cotangent = jnp.concatenate([cotangent_ref[b] for b in range(tile_blocks)], 1).astype(F32)
    grad = (cotangent * gate * (1.0 + preact * (1.0 - gate))).astype(BF16)
    folded = jnp.concatenate([grad[:, :span], grad[:, span:]], 0)
    for first in range(0, offsets, chunk):
        ks = range(first, first + chunk)
        rows = [table_row(target_ref, k) for k in ks]
        table = jnp.concatenate([one_hot(r & (span - 1), span) for r in rows], 1)
        gathered = jnp.dot(folded, table, preferred_element_type=F32).astype(BF16)
        for n, k in enumerate(ks):
            inside = slice(n * width, (n + 1) * width)
            lanes = slice(k * width, (k + 1) * width)
            fold = (rows[n] // span).astype(F32).astype(BF16)
            picked = pick_fold(fold, [gathered[:channels, inside], gathered[channels:, inside]])
            grad_columns_ref[:, lanes] = picked
            term = lax.dot_general(
                columns_ref[:, lanes],
                picked,
                (((1,), (1,)), ((), ())),
                preferred_element_type=F32,
            )
            row = (k % portion) * half
            held[(k // portion) ^ here, row : row + half, :] = term
    for n, ref in enumerate(portions):
        ref[...] = held[n].astype(ref.dtype)
    start = pl.multiple_of(lax.axis_index("chan") * half, half)
    own = part_ref[pl.ds(start, half), :] + other_ref[pl.ds(start, half), :]
    own = own / (1.0 + jnp.exp(-own))
    for b in range(tile_blocks):
        act_ref[b] = own[:, b * width : (b + 1) * width].astype(BF16)


def input_grad_kernel(grad_columns_ref, source_ref, weight_ref, own_ref, *refs):
    rims, (values, places) = refs[:-2], refs[-2:]
    tile_blocks = own_ref.shape[0]
    offsets, half, _ = weight_ref.shape
    width = source_ref.shape[1]
    span = 2 * width
    folds = values.shape[0] // half
    for k in range(offsets):
        lanes = slice(k * width, (k + 1) * width)
        returned = jnp.dot(
            weight_ref[k], grad_columns_ref[:, lanes], preferred_element_type=F32
        ).astype(BF16)
        source = table_row(source_ref, k)
        fold = (source // span).astype(F32).astype(BF16)
        places[:, lanes] = one_hot(source & (span - 1), span)
        for f in range(folds):
            values[f * half : (f + 1) * half, lanes] = mask_fold(fold, f, returned)
    total = lax.dot_general(
        values[...], places[...], (((1,), (1,)), ((), ())), preferred_element_type=F32
    )

    def block(b):
        return total[(b // 2) * half : (b // 2 + 1) * half, (b % 2) * width : (b % 2 + 1) * width]

    for b in range(tile_blocks):
        own_ref[b] = block(b)
    place = tile_blocks
    for rim in rims:
        for b in range(rim.shape[0]):
            rim[b] = block(place).astype(BF16)
            place += 1


def add_rims(swaps, halo_ref, total, received):
    for (axis, parity, _), ref in zip(swaps, received):
        group = direction(axis, parity)
        for b in range(ref.shape[0]):
            where = halo_ref[group, b]
            total[where] = total[where] + ref[b].astype(F32)


def tile_grad_kernel(swaps, halo_ref, own_ref, *refs):
    received, (out_ref, total) = refs[:-2], refs[-2:]
    total[...] = own_ref[...]
    add_rims(swaps, halo_ref, total, received)
    out_ref[...] = total[...].astype(BF16)


def collect_kernel(swaps, halo_ref, own_ref, keep_ref, crossed_ref, *refs):
    received, refs = refs[: len(swaps)], refs[len(swaps) :]
    (grad_ref, share_ref, *sends), (total, terms) = refs[:-2], refs[-2:]
    blocks, half, _ = own_ref.shape
    terms[...] = keep_ref[...] + crossed_ref[...].astype(F32)
    total[...] = own_ref[...]
    add_rims(swaps, halo_ref, total, received)
    for b in range(blocks):
        grad_ref[b * half : (b + 1) * half, :] = total[b].astype(BF16)
    i = lax.axis_index("tile")
    rows = share_ref.shape[0]
    for d, ref in enumerate((share_ref, *sends)):
        share = terms[pl.ds(pl.multiple_of((i ^ d) * rows, rows), rows), :]
        if d:
            ref[: blocks * half, :] = grad_ref[...]
            ref[blocks * half :, :] = share.astype(BF16)
        else:
            ref[...] = share


def column_kernel(early, share_ref, *refs):
    received, (bulk_ref, shard_ref) = refs[:-2], refs[-2:]
    rows = received[0].shape[0] - share_ref.shape[0]
    total = share_ref[...]
    for d, ref in enumerate(received):
        total = total + ref[rows:, :].astype(F32)
        if d >= early:
            bulk_ref[(d - early) * rows : (d - early + 1) * rows, :] = ref[:rows, :]
    shard_ref[...] = total.astype(BF16)
    bulk_ref[(len(received) - early) * rows :, :] = shard_ref[...]


def spread_kernel(place_ref, *refs):
    parts, (out_ref, held) = refs[:-2], refs[-2:]
    height = out_ref.shape[1]
    rows = parts[0].shape[0]
    first = 0
    for n, ref in enumerate(parts):
        count = rows if n % 3 < 2 else held.shape[0] // 2 - 2 * rows
        held[first : first + count, :] = ref[:count, :]
        first += count
    for b in range(out_ref.shape[0]):
        start = pl.multiple_of(place_ref[b] * height, height)
        out_ref[b] = held[pl.ds(start, height), :]


def weight_kernel(scale, tile_rows, *refs):
    near, (bulk_ref, *far), (out_ref, held) = refs[:tile_rows], refs[tile_rows:-2], refs[-2:]
    i, j = lax.axis_index("tile"), lax.axis_index("depth")
    rows = near[0].shape[0]
    for jx in range(2):
        for d in range(tile_rows):
            if jx == 0:
                shard = near[d][...]
            elif d == 0:
                shard = bulk_ref[bulk_ref.shape[0] - rows :, :]
            else:
                shard = far[d - 1][...]
            start = pl.multiple_of(((j ^ jx) * tile_rows + (i ^ d)) * rows, rows)
            held[pl.ds(start, rows), :] = shard.astype(F32) * scale
    out_ref[...] = held[: out_ref.shape[0], :]


def swap_all(swaps, arrays):
    return [
        lax.ppermute(array, axis, pairs) for (axis, _, pairs), array in zip(swaps, arrays)
    ]


def to_rows(arrays, tile_rows):
    return [arrays[0]] + [
        lax.ppermute(arrays[d], "tile", xor_pairs(tile_rows, d)) for d in range(1, tile_rows)
    ]


def across(array):
    return lax.ppermute(array, "depth", [(0, 1), (1, 0)])


def relay(outgoing):
    return lax.all_to_all(outgoing, TILES_AXES, split_axis=0, concat_axis=0, tiled=True)


def local(
    log_features, send_slot, merge_slot, halo_list, in_rows, out_rows, pair_count, weight, cotangent
):
    tile_rows = lax.axis_size("tile")
    depths = lax.axis_size("depth")
    tile_count = tile_rows * depths
    log_blocks = log_features[0]
    log_count, half, width = log_blocks.shape
    tile_blocks = cotangent.shape[1]
    offsets, channels, _ = weight.shape
    capacity = send_slot.shape[2]
    rim_count = halo_list.shape[2]
    pair_slots = in_rows.shape[2]
    own_total = tile_blocks * width
    span = 2 * width
    chunk = 28
    padded = -(-offsets // chunk) * chunk
    swaps = exchanges(tile_rows, depths)
    merged = (tile_rows, depths) == (4, 2) and capacity >= tile_blocks
    send, merge, halo = send_slot[0], merge_slot[0], halo_list[0]

    block_of = in_rows[0] // width
    group_of = (block_of - tile_blocks) // rim_count
    held_total = tile_blocks + len(swaps) * rim_count
    new_block = jnp.where(block_of < tile_blocks, block_of, held_total)
    for place, (axis, parity, _) in enumerate(swaps):
        hit = (block_of >= tile_blocks) & (group_of == direction(axis, parity))
        inside = (block_of - tile_blocks) % rim_count
        new_block = jnp.where(hit, tile_blocks + place * rim_count + inside, new_block)
    live = jnp.arange(pair_slots, dtype=jnp.int32)[None, :] < pair_count[0][:, None]
    source_rows = jnp.where(live, new_block * width + in_rows[0] % width, held_total * width)
    target_rows = jnp.where(live, out_rows[0], own_total)
    extra = ((0, padded - offsets), (0, 0))
    source_rows = jnp.pad(source_rows, extra, constant_values=held_total * width)
    target_rows = jnp.pad(target_rows, extra, constant_values=own_total)
    w_rows = lax.dynamic_slice_in_dim(weight, lax.axis_index("chan") * half, half, 1)
    w_rows = jnp.pad(w_rows, ((0, padded - offsets), (0, 0), (0, 0)))
    w_rows_t = w_rows.transpose(0, 2, 1)
    cotangent_full = lax.all_gather(cotangent[0], "chan", axis=1, tiled=True)

    rim_shape = shape((rim_count, half, width), BF16)
    block_shape = shape((tile_blocks, half, width), BF16)
    if merged:
        near = to_rows([merge] * tile_rows, tile_rows)
        log_blocks = pl.pallas_call(
            copy_kernel,
            out_shape=shape(log_blocks.shape, BF16),
            in_specs=[VMEM],
            out_specs=VMEM,
            compiler_params=PARAMS,
        )(log_blocks)
        stacked, log_blocks = lax.optimization_barrier((jnp.stack(near), log_blocks))
        far = across(stacked)
        held_blocks = (tile_rows // 2 * tile_blocks, half, width)
        def far_sums(rows_away):
            return across(
                pl.pallas_call(
                    functools.partial(far_kernel, rows_away, depths, tile_blocks),
                    out_shape=shape(held_blocks, BF16),
                    in_specs=[SMEM] * 2 + [VMEM],
                    out_specs=VMEM,
                    compiler_params=PARAMS,
                )(send, far, log_blocks)
            )

        far_high = far_sums(range(tile_rows // 2, tile_rows))
        far_low = far_sums(range(tile_rows // 2))
        near_low, near_high = pl.pallas_call(
            functools.partial(near_kernel, tile_rows, depths, tile_blocks),
            out_shape=(shape(held_blocks, F32),) * 2,
            in_specs=[SMEM] * (1 + tile_rows) + [VMEM],
            out_specs=(VMEM,) * 2,
            compiler_params=PARAMS,
        )(send, *near, log_blocks)
        place = pl.pallas_call(
            functools.partial(place_kernel, tile_rows, depths, tile_blocks),
            out_shape=shape((log_count + 1,), jnp.int32),
            in_specs=[SMEM] * (2 + tile_rows),
            out_specs=SMEM,
            compiler_params=PARAMS,
        )(send, *near, far)
        add = functools.partial(
            pl.pallas_call,
            add_kernel,
            in_specs=[VMEM] * 2,
            out_specs=(VMEM,) * 2,
            compiler_params=PARAMS,
        )
        high = add(out_shape=(block_shape,) * 2)(near_high, far_high)
        low = add(out_shape=(shape((tile_blocks, half, width), F32), block_shape))(
            near_low, far_low
        )
        incoming = to_rows([*low, *high], tile_rows)
        incoming, place = lax.optimization_barrier((incoming, place))
    else:
        pick_table = (
            send.reshape(-1)[:, None] == jnp.arange(log_count, dtype=jnp.int32)[None, :]
        ).astype(BF16)
        outgoing = jnp.dot(
            pick_table, log_blocks.reshape(log_count, half * width), preferred_element_type=F32
        ).astype(BF16)
        incoming = relay(outgoing.reshape(tile_count, capacity, half, width))
        place_table = (
            jnp.arange(tile_blocks, dtype=jnp.int32)[:, None] == merge.reshape(-1)[None, :]
        ).astype(BF16)
        incoming = jnp.dot(
            place_table,
            incoming.reshape(tile_count * capacity, half * width),
            preferred_element_type=F32,
        )
        incoming = [incoming.astype(BF16).reshape(tile_blocks, half, width)]
    features, *sends = pl.pallas_call(
        functools.partial(merge_kernel, swaps),
        out_shape=(block_shape,) + (rim_shape,) * len(swaps),
        in_specs=[SMEM] + [VMEM] * len(incoming),
        out_specs=(VMEM,) * (1 + len(swaps)),
        compiler_params=PARAMS,
    )(halo, *incoming)
    received = swap_all(swaps, sends)

    pairs_total = padded * pair_slots
    own_columns = pl.pallas_call(
        functools.partial(own_columns_kernel, chunk),
        out_shape=shape((half, pairs_total), BF16),
        in_specs=[VMEM] * 2,
        out_specs=VMEM,
        compiler_params=PARAMS,
    )(features, source_rows)
    part, columns = pl.pallas_call(
        functools.partial(forward_kernel, tile_blocks // 2, chunk),
        out_shape=(shape((channels, own_total), F32), shape((half, pairs_total), BF16)),
        in_specs=[VMEM] * (4 + len(swaps)),
        out_specs=(VMEM, VMEM),
        scratch_shapes=[
            pltpu.VMEM((2 * channels, pairs_total), BF16),
            pltpu.VMEM((span, pairs_total), BF16),
        ],
        compiler_params=PARAMS,
    )(own_columns, source_rows, target_rows, w_rows_t, *received)
    other = lax.ppermute(part, "chan", [(0, 1), (1, 0)])

    portions = depths if merged else 1
    portion = (padded // portions * half, channels)
    activations, grad_columns, keep, *cross = pl.pallas_call(
        functools.partial(weight_grad_kernel, chunk // 2),
        out_shape=(block_shape, shape((channels, pairs_total), BF16), shape(portion, F32))
        + (shape(portion, BF16),) * (portions - 1),
        in_specs=[VMEM] * 5,
        out_specs=(VMEM,) * (2 + portions),
        scratch_shapes=[pltpu.VMEM((portions, *portion), F32)],
        compiler_params=PARAMS,
    )(part, other, cotangent_full, target_rows, columns)
    scale = float(tile_count * pair_slots) ** (-0.5)
    own_grad, *rims = pl.pallas_call(
        input_grad_kernel,
        out_shape=(shape((tile_blocks, half, width), F32),) + (rim_shape,) * len(swaps),
        in_specs=[VMEM] * 3,
        out_specs=(VMEM,) * (1 + len(swaps)),
        scratch_shapes=[
            pltpu.VMEM((held_total // 2 * half, pairs_total), BF16),
            pltpu.VMEM((span, pairs_total), BF16),
        ],
        compiler_params=PARAMS,
    )(grad_columns, source_rows, w_rows)
    returned = swap_all(swaps, rims)
    if merged:
        rows = portion[0] // tile_rows
        own_rows = tile_blocks * half
        column_rows = tile_rows * own_rows
        grad, share, *sends = pl.pallas_call(
            functools.partial(collect_kernel, swaps),
            out_shape=(shape((own_rows, width), BF16), shape((rows, channels), F32))
            + (shape((own_rows + rows, width), BF16),) * (tile_rows - 1),
            in_specs=[SMEM] + [VMEM] * (3 + len(swaps)),
            out_specs=(VMEM,) * (1 + tile_rows),
            scratch_shapes=[
                pltpu.VMEM((tile_blocks, half, width), F32),
                pltpu.VMEM(portion, F32),
            ],
            compiler_params=PARAMS,
        )(halo, own_grad, keep, across(cross[0]), *returned)
        received = to_rows([share, *sends], tile_rows)
        early = [across(grad), across(received[1])]
        received, early = lax.optimization_barrier((received, early))
        bulk, shard = pl.pallas_call(
            functools.partial(column_kernel, 1),
            out_shape=(
                shape((column_rows - 2 * own_rows + rows, channels), BF16),
                shape((rows, channels), BF16),
            ),
            in_specs=[VMEM] * tile_rows,
            out_specs=(VMEM,) * 2,
            compiler_params=PARAMS,
        )(*received)
        other_bulk = across(bulk)
        shards = to_rows([shard] * tile_rows, tile_rows)
        grad_log = pl.pallas_call(
            spread_kernel,
            out_shape=shape((log_count, half, width), BF16),
            in_specs=[SMEM] + [VMEM] * 6,
            out_specs=VMEM,
            scratch_shapes=[pltpu.VMEM((2 * column_rows, width), BF16)],
            compiler_params=PARAMS,
        )(place, grad, received[1], bulk, *early, other_bulk)
        far_shards = [across(part) for part in shards[1:]]
        far_shards, grad_log = lax.optimization_barrier((far_shards, grad_log))
        grad_weight = pl.pallas_call(
            functools.partial(weight_kernel, scale, tile_rows),
            out_shape=shape((offsets * half, channels), F32),
            in_specs=[VMEM] * (2 * tile_rows),
            out_specs=VMEM,
            scratch_shapes=[pltpu.VMEM((padded * half, channels), F32)],
            compiler_params=PARAMS,
        )(*shards, other_bulk, *far_shards)
    else:
        tile_grad = pl.pallas_call(
            functools.partial(tile_grad_kernel, swaps),
            out_shape=block_shape,
            in_specs=[SMEM] + [VMEM] * (1 + len(swaps)),
            out_specs=VMEM,
            scratch_shapes=[pltpu.VMEM((tile_blocks, half, width), F32)],
            compiler_params=PARAMS,
        )(halo, own_grad, *returned)
        back_blocks = jnp.dot(
            place_table.T,
            tile_grad.reshape(tile_blocks, half * width),
            preferred_element_type=F32,
        ).astype(BF16)
        back = relay(back_blocks.reshape(tile_count, capacity, half, width))
        grad_log = jnp.dot(
            pick_table.T,
            back.reshape(tile_count * capacity, half * width),
            preferred_element_type=F32,
        ).astype(BF16)
        grad_weight = lax.psum(keep[: offsets * half], TILES_AXES) * scale
    return (
        activations[None],
        grad_log.reshape(1, log_count, half, width),
        grad_weight.reshape(offsets, half, channels),
    )


def solution(mesh):
    split = ("groups", "tile", "depth")
    in_specs = (
        P(split, None, "chan", None),
        P(split, None, None),
        P(split, None, None),
        P(split, None, None),
        P(split, None, None),
        P(split, None, None),
        P(split, None),
        P(),
        P(split, None, "chan", None),
    )
    out_specs = (
        P(split, None, "chan", None),
        P(split, None, "chan", None),
        P("groups", "chan", None),
    )
    return jax.shard_map(local, mesh=mesh, in_specs=in_specs, out_specs=out_specs, check_vma=False)
```

```python
import functools

import jax
import jax.numpy as jnp
from jax import lax
from jax.experimental import pallas as pl
from jax.experimental.pallas import tpu as pltpu
from jax.sharding import PartitionSpec as P

F32 = jnp.float32
BF16 = jnp.bfloat16
TILES_AXES = ("tile", "depth")
VMEM = pl.BlockSpec(memory_space=pltpu.VMEM)
SMEM = pl.BlockSpec(memory_space=pltpu.SMEM)
PARAMS = pltpu.CompilerParams(vmem_limit_bytes=24 * 1024 * 1024)


def shape(dims, dtype):
    return jax.ShapeDtypeStruct(dims, dtype)


def pair_lists(size):
    return [
        [pair for i in range(first, size - 1, 2) for pair in ((i, i + 1), (i + 1, i))]
        for first in (0, 1)
    ]


def exchanges(tile_rows, depths):
    found = []
    for axis, size in (("tile", tile_rows), ("depth", depths)):
        for parity, pairs in enumerate(pair_lists(size)):
            if pairs:
                found.append((axis, parity, pairs))
    return found


def direction(axis, parity):
    place = lax.axis_index(axis) % 2
    upper = (place == parity).astype(jnp.int32)
    return upper + (0 if axis == "tile" else 2)


def xor_pairs(size, distance):
    return [(i, i ^ distance) for i in range(size)]


def merge_column(jx, rows_away, depths, tile_blocks, send_ref, tables, log_ref, emit):
    i, j = lax.axis_index("tile"), lax.axis_index("depth")
    me = i * depths + j
    half, width = log_ref.shape[1:]
    for d in rows_away:
        p = (i ^ d) * depths + (j ^ jx)
        totals = [jnp.zeros((half, width), F32) for _ in range(tile_blocks)]
        for c in range(send_ref.shape[1]):
            block = send_ref[p, c]
            wanted = jnp.where(block >= 0, tables(d, me, c), -1)
            rows = log_ref[jnp.maximum(block, 0)].astype(F32)
            for m in range(tile_blocks):
                totals[m] = totals[m] + rows * jnp.where(wanted == m, 1.0, 0.0)
        for m in range(tile_blocks):
            emit(d, m, totals[m])


def copy_kernel(in_ref, out_ref):
    out_ref[...] = in_ref[...]


def far_kernel(rows_away, depths, tile_blocks, send_ref, far_ref, log_ref, out_ref):
    def emit(d, m, total):
        out_ref[(d - rows_away[0]) * tile_blocks + m] = total.astype(BF16)

    merge_column(
        1, rows_away, depths, tile_blocks, send_ref, lambda *at: far_ref[at], log_ref, emit
    )


def near_kernel(tile_rows, depths, tile_blocks, *refs):
    send_ref, tables, log_ref, outs = refs[0], refs[1:-3], refs[-3], refs[-2:]
    per = tile_rows // len(outs)

    def emit(d, m, total):
        outs[d // per][(d % per) * tile_blocks + m] = total

    merge_column(
        0,
        range(tile_rows),
        depths,
        tile_blocks,
        send_ref,
        lambda d, *at: tables[d][at],
        log_ref,
        emit,
    )


def place_kernel(tile_rows, depths, tile_blocks, *refs):
    send_ref, tables, far_ref, place_ref = refs[0], refs[1:-2], refs[-2], refs[-1]
    i, j = lax.axis_index("tile"), lax.axis_index("depth")
    me = i * depths + j
    for jx in range(depths):
        for d in range(tile_rows):
            p = (i ^ d) * depths + (j ^ jx)
            for c in range(send_ref.shape[1]):
                block = send_ref[p, c]
                target = far_ref[d, me, c] if jx else tables[d][me, c]
                spot = jnp.where(block >= 0, block, place_ref.shape[0] - 1)
                place_ref[spot] = (jx * tile_rows + d) * tile_blocks + target


def add_kernel(near_ref, far_ref, *outs):
    count = near_ref.shape[0] // len(outs)
    for n, ref in enumerate(outs):
        for m in range(count):
            at = n * count + m
            ref[m] = (near_ref[at] + far_ref[at].astype(F32)).astype(ref.dtype)


def merge_kernel(swaps, halo_ref, *refs):
    incoming, features_ref = refs[: -1 - len(swaps)], refs[-1 - len(swaps)]
    sends = refs[-len(swaps) :] if swaps else ()
    for m in range(features_ref.shape[0]):
        total = incoming[0][m].astype(F32)
        for ref in incoming[1:]:
            total = total + ref[m].astype(F32)
        features_ref[m] = total.astype(BF16)
    pick_blocks(swaps, features_ref, halo_ref, sends)


def pick_blocks(swaps, features_ref, halo_ref, sends):
    for (axis, parity, _), send_ref in zip(swaps, sends):
        group = direction(axis, parity)
        for b in range(send_ref.shape[0]):
            send_ref[b] = features_ref[halo_ref[group, b]]


def table_row(ref, k):
    return ref[k : k + 1, :]


def one_hot(low, height):
    rows = lax.broadcasted_iota(jnp.int32, (height, low.shape[1]), 0).astype(F32).astype(BF16)
    low = low.astype(F32).astype(BF16)
    return jnp.where(rows == low, jnp.ones((), BF16), jnp.zeros((), BF16))


def pick_fold(fold, parts):
    picked = jnp.zeros_like(parts[0])
    for f, part in enumerate(parts):
        picked = jnp.where(fold == f, part, picked)
    return picked


def mask_fold(fold, f, part):
    return jnp.where(fold == f, part, jnp.zeros_like(part))


def gather_folds(folded, rows_ref, first_fold, chunk, half, base_of, emit):
    offsets, width = rows_ref.shape
    span = 2 * width
    for first in range(0, offsets, chunk):
        rows = [table_row(rows_ref, k) for k in range(first, first + chunk)]
        table = jnp.concatenate([one_hot(r & (span - 1), span) for r in rows], 1)
        gathered = jnp.dot(folded, table, preferred_element_type=F32).astype(BF16)
        for n, row in enumerate(rows):
            fold = (row // span).astype(F32).astype(BF16)
            picked = base_of(first + n)
            for f in range(folded.shape[0] // half):
                part = gathered[f * half : (f + 1) * half, n * width : (n + 1) * width]
                picked = jnp.where(fold == first_fold + f, part, picked)
            emit(first + n, picked)


def fold_blocks(blocks):
    return jnp.concatenate(
        [jnp.concatenate(blocks[n : n + 2], 1) for n in range(0, len(blocks), 2)], 0
    )


def own_columns_kernel(chunk, features_ref, source_ref, out_ref):
    count, half, width = features_ref.shape
    zero = jnp.zeros((half, width), BF16)

    def emit(k, picked):
        out_ref[:, k * width : (k + 1) * width] = picked

    folded = fold_blocks([features_ref[b] for b in range(count)])
    gather_folds(folded, source_ref, 0, chunk, half, lambda k: zero, emit)


def forward_kernel(own_folds, chunk, *refs):
    own_ref, source_ref, target_ref, weight_ref = refs[:4]
    received, (part_ref, columns_ref, values, places) = refs[4:-4], refs[-4:]
    channels, half = weight_ref.shape[1:]
    offsets, width = source_ref.shape
    span = 2 * width

    def lanes(k):
        return slice(k * width, (k + 1) * width)

    def emit(k, picked):
        columns_ref[:, lanes(k)] = picked

    def multiply(k):
        product = jnp.dot(weight_ref[k], columns_ref[:, lanes(k)], preferred_element_type=F32)
        product = product.astype(BF16)
        target = table_row(target_ref, k)
        fold = (target // span).astype(F32).astype(BF16)
        places[:, lanes(k)] = one_hot(target & (span - 1), span)
        for f in range(2):
            values[f * channels : (f + 1) * channels, lanes(k)] = mask_fold(fold, f, product)

    blocks = [ref[b] for ref in received for b in range(ref.shape[0])]
    if blocks:
        gather_folds(
            fold_blocks(blocks),
            source_ref,
            own_folds,
            chunk,
            half,
            lambda k: own_ref[:, lanes(k)],
            emit,
        )
    else:
        for k in range(offsets):
            emit(k, own_ref[:, lanes(k)])
    for k in range(offsets):
        multiply(k)
    total = lax.dot_general(
        values[...], places[...], (((1,), (1,)), ((), ())), preferred_element_type=F32
    )
    part_ref[:, :span] = total[:channels]
    part_ref[:, span:] = total[channels:]


def weight_grad_kernel(chunk, *refs):
    part_ref, other_ref, cotangent_ref, target_ref, columns_ref = refs[:5]
    act_ref, grad_columns_ref = refs[5:7]
    portions, held = refs[7:-1], refs[-1]
    tile_blocks, channels, width = cotangent_ref.shape
    half = columns_ref.shape[0]
    offsets = target_ref.shape[0]
    span = 2 * width
    portion = offsets // len(portions)
    here = lax.axis_index("depth") if len(portions) > 1 else 0
    preact = part_ref[...] + other_ref[...]
    gate = 1.0 / (1.0 + jnp.exp(-preact))
    cotangent = jnp.concatenate([cotangent_ref[b] for b in range(tile_blocks)], 1).astype(F32)
    grad = (cotangent * gate * (1.0 + preact * (1.0 - gate))).astype(BF16)
    folded = jnp.concatenate([grad[:, :span], grad[:, span:]], 0)
    for first in range(0, offsets, chunk):
        ks = range(first, first + chunk)
        rows = [table_row(target_ref, k) for k in ks]
        table = jnp.concatenate([one_hot(r & (span - 1), span) for r in rows], 1)
        gathered = jnp.dot(folded, table, preferred_element_type=F32).astype(BF16)
        for n, k in enumerate(ks):
            inside = slice(n * width, (n + 1) * width)
            lanes = slice(k * width, (k + 1) * width)
            fold = (rows[n] // span).astype(F32).astype(BF16)
            picked = pick_fold(fold, [gathered[:channels, inside], gathered[channels:, inside]])
            grad_columns_ref[:, lanes] = picked
    for k in range(offsets):
        lanes = slice(k * width, (k + 1) * width)
        row = (k % portion) * half
        held[(k // portion) ^ here, row : row + half, :] = lax.dot_general(
            columns_ref[:, lanes],
            grad_columns_ref[:, lanes],
            (((1,), (1,)), ((), ())),
            preferred_element_type=F32,
        )
    for n, ref in enumerate(portions):
        ref[...] = held[n].astype(ref.dtype)
    start = pl.multiple_of(lax.axis_index("chan") * half, half)
    own = part_ref[pl.ds(start, half), :] + other_ref[pl.ds(start, half), :]
    own = own / (1.0 + jnp.exp(-own))
    for b in range(tile_blocks):
        act_ref[b] = own[:, b * width : (b + 1) * width].astype(BF16)


def input_grad_kernel(grad_columns_ref, source_ref, weight_ref, own_ref, *refs):
    rims, (values, places) = refs[:-2], refs[-2:]
    tile_blocks = own_ref.shape[0]
    offsets, half, _ = weight_ref.shape
    width = source_ref.shape[1]
    span = 2 * width
    folds = values.shape[0] // half
    for k in range(offsets):
        lanes = slice(k * width, (k + 1) * width)
        returned = jnp.dot(
            weight_ref[k], grad_columns_ref[:, lanes], preferred_element_type=F32
        ).astype(BF16)
        source = table_row(source_ref, k)
        fold = (source // span).astype(F32).astype(BF16)
        places[:, lanes] = one_hot(source & (span - 1), span)
        for f in range(folds):
            values[f * half : (f + 1) * half, lanes] = mask_fold(fold, f, returned)
    total = lax.dot_general(
        values[...], places[...], (((1,), (1,)), ((), ())), preferred_element_type=F32
    )

    def block(b):
        return total[(b // 2) * half : (b // 2 + 1) * half, (b % 2) * width : (b % 2 + 1) * width]

    for b in range(tile_blocks):
        own_ref[b] = block(b)
    place = tile_blocks
    for rim in rims:
        for b in range(rim.shape[0]):
            rim[b] = block(place).astype(BF16)
            place += 1


def add_rims(swaps, halo_ref, total, received):
    for (axis, parity, _), ref in zip(swaps, received):
        group = direction(axis, parity)
        for b in range(ref.shape[0]):
            where = halo_ref[group, b]
            total[where] = total[where] + ref[b].astype(F32)


def tile_grad_kernel(swaps, halo_ref, own_ref, *refs):
    received, (out_ref, total) = refs[:-2], refs[-2:]
    total[...] = own_ref[...]
    add_rims(swaps, halo_ref, total, received)
    out_ref[...] = total[...].astype(BF16)


def collect_kernel(swaps, halo_ref, own_ref, keep_ref, crossed_ref, *refs):
    received, refs = refs[: len(swaps)], refs[len(swaps) :]
    (grad_ref, share_ref, *sends), (total, terms) = refs[:-2], refs[-2:]
    blocks, half, _ = own_ref.shape
    terms[...] = keep_ref[...] + crossed_ref[...].astype(F32)
    total[...] = own_ref[...]
    add_rims(swaps, halo_ref, total, received)
    for b in range(blocks):
        grad_ref[b * half : (b + 1) * half, :] = total[b].astype(BF16)
    i = lax.axis_index("tile")
    rows = share_ref.shape[0]
    for d, ref in enumerate((share_ref, *sends)):
        share = terms[pl.ds(pl.multiple_of((i ^ d) * rows, rows), rows), :]
        if d:
            ref[: blocks * half, :] = grad_ref[...]
            ref[blocks * half :, :] = share.astype(BF16)
        else:
            ref[...] = share


def column_kernel(early, share_ref, *refs):
    received, (bulk_ref, shard_ref) = refs[:-2], refs[-2:]
    rows = received[0].shape[0] - share_ref.shape[0]
    total = share_ref[...]
    for d, ref in enumerate(received):
        total = total + ref[rows:, :].astype(F32)
        if d >= early:
            bulk_ref[(d - early) * rows : (d - early + 1) * rows, :] = ref[:rows, :]
    shard_ref[...] = total.astype(BF16)
    bulk_ref[(len(received) - early) * rows :, :] = shard_ref[...]


def spread_kernel(place_ref, *refs):
    parts, (out_ref, held) = refs[:-2], refs[-2:]
    height = out_ref.shape[1]
    rows = parts[0].shape[0]
    first = 0
    for n, ref in enumerate(parts):
        count = rows if n % 3 < 2 else held.shape[0] // 2 - 2 * rows
        held[first : first + count, :] = ref[:count, :]
        first += count
    for b in range(out_ref.shape[0]):
        start = pl.multiple_of(place_ref[b] * height, height)
        out_ref[b] = held[pl.ds(start, height), :]


def weight_kernel(scale, tile_rows, *refs):
    near, (bulk_ref, *far), (out_ref, held) = refs[:tile_rows], refs[tile_rows:-2], refs[-2:]
    i, j = lax.axis_index("tile"), lax.axis_index("depth")
    rows = near[0].shape[0]
    for jx in range(2):
        for d in range(tile_rows):
            if jx == 0:
                shard = near[d][...]
            elif d == 0:
                shard = bulk_ref[bulk_ref.shape[0] - rows :, :]
            else:
                shard = far[d - 1][...]
            start = pl.multiple_of(((j ^ jx) * tile_rows + (i ^ d)) * rows, rows)
            held[pl.ds(start, rows), :] = shard.astype(F32) * scale
    out_ref[...] = held[: out_ref.shape[0], :]


def swap_all(swaps, arrays):
    return [
        lax.ppermute(array, axis, pairs) for (axis, _, pairs), array in zip(swaps, arrays)
    ]


def to_rows(arrays, tile_rows):
    return [arrays[0]] + [
        lax.ppermute(arrays[d], "tile", xor_pairs(tile_rows, d)) for d in range(1, tile_rows)
    ]


def across(array):
    return lax.ppermute(array, "depth", [(0, 1), (1, 0)])


def relay(outgoing):
    return lax.all_to_all(outgoing, TILES_AXES, split_axis=0, concat_axis=0, tiled=True)


def local(
    log_features, send_slot, merge_slot, halo_list, in_rows, out_rows, pair_count, weight, cotangent
):
    tile_rows = lax.axis_size("tile")
    depths = lax.axis_size("depth")
    tile_count = tile_rows * depths
    log_blocks = log_features[0]
    log_count, half, width = log_blocks.shape
    tile_blocks = cotangent.shape[1]
    offsets, channels, _ = weight.shape
    capacity = send_slot.shape[2]
    rim_count = halo_list.shape[2]
    pair_slots = in_rows.shape[2]
    own_total = tile_blocks * width
    span = 2 * width
    chunk = 28
    padded = -(-offsets // chunk) * chunk
    swaps = exchanges(tile_rows, depths)
    merged = (tile_rows, depths) == (4, 2) and capacity >= tile_blocks
    send, merge, halo = send_slot[0], merge_slot[0], halo_list[0]

    block_of = in_rows[0] // width
    group_of = (block_of - tile_blocks) // rim_count
    held_total = tile_blocks + len(swaps) * rim_count
    new_block = jnp.where(block_of < tile_blocks, block_of, held_total)
    for place, (axis, parity, _) in enumerate(swaps):
        hit = (block_of >= tile_blocks) & (group_of == direction(axis, parity))
        inside = (block_of - tile_blocks) % rim_count
        new_block = jnp.where(hit, tile_blocks + place * rim_count + inside, new_block)
    live = jnp.arange(pair_slots, dtype=jnp.int32)[None, :] < pair_count[0][:, None]
    source_rows = jnp.where(live, new_block * width + in_rows[0] % width, held_total * width)
    target_rows = jnp.where(live, out_rows[0], own_total)
    extra = ((0, padded - offsets), (0, 0))
    source_rows = jnp.pad(source_rows, extra, constant_values=held_total * width)
    target_rows = jnp.pad(target_rows, extra, constant_values=own_total)
    w_rows = lax.dynamic_slice_in_dim(weight, lax.axis_index("chan") * half, half, 1)
    w_rows = jnp.pad(w_rows, ((0, padded - offsets), (0, 0), (0, 0)))
    w_rows_t = w_rows.transpose(0, 2, 1)
    cotangent_full = lax.all_gather(cotangent[0], "chan", axis=1, tiled=True)

    rim_shape = shape((rim_count, half, width), BF16)
    block_shape = shape((tile_blocks, half, width), BF16)
    if merged:
        near = to_rows([merge] * tile_rows, tile_rows)
        log_blocks = pl.pallas_call(
            copy_kernel,
            out_shape=shape(log_blocks.shape, BF16),
            in_specs=[VMEM],
            out_specs=VMEM,
            compiler_params=PARAMS,
        )(log_blocks)
        stacked, log_blocks = lax.optimization_barrier((jnp.stack(near), log_blocks))
        far = across(stacked)
        held_blocks = (tile_rows // 2 * tile_blocks, half, width)
        def far_sums(rows_away):
            return across(
                pl.pallas_call(
                    functools.partial(far_kernel, rows_away, depths, tile_blocks),
                    out_shape=shape(held_blocks, BF16),
                    in_specs=[SMEM] * 2 + [VMEM],
                    out_specs=VMEM,
                    compiler_params=PARAMS,
                )(send, far, log_blocks)
            )

        far_high = far_sums(range(tile_rows // 2, tile_rows))
        far_low = far_sums(range(tile_rows // 2))
        near_low, near_high = pl.pallas_call(
            functools.partial(near_kernel, tile_rows, depths, tile_blocks),
            out_shape=(shape(held_blocks, F32),) * 2,
            in_specs=[SMEM] * (1 + tile_rows) + [VMEM],
            out_specs=(VMEM,) * 2,
            compiler_params=PARAMS,
        )(send, *near, log_blocks)
        place = pl.pallas_call(
            functools.partial(place_kernel, tile_rows, depths, tile_blocks),
            out_shape=shape((log_count + 1,), jnp.int32),
            in_specs=[SMEM] * (2 + tile_rows),
            out_specs=SMEM,
            compiler_params=PARAMS,
        )(send, *near, far)
        add = functools.partial(
            pl.pallas_call,
            add_kernel,
            in_specs=[VMEM] * 2,
            out_specs=(VMEM,) * 2,
            compiler_params=PARAMS,
        )
        high = add(out_shape=(block_shape,) * 2)(near_high, far_high)
        low = add(out_shape=(shape((tile_blocks, half, width), F32), block_shape))(
            near_low, far_low
        )
        incoming = to_rows([*low, *high], tile_rows)
        incoming, place = lax.optimization_barrier((incoming, place))
    else:
        pick_table = (
            send.reshape(-1)[:, None] == jnp.arange(log_count, dtype=jnp.int32)[None, :]
        ).astype(BF16)
        outgoing = jnp.dot(
            pick_table, log_blocks.reshape(log_count, half * width), preferred_element_type=F32
        ).astype(BF16)
        incoming = relay(outgoing.reshape(tile_count, capacity, half, width))
        place_table = (
            jnp.arange(tile_blocks, dtype=jnp.int32)[:, None] == merge.reshape(-1)[None, :]
        ).astype(BF16)
        incoming = jnp.dot(
            place_table,
            incoming.reshape(tile_count * capacity, half * width),
            preferred_element_type=F32,
        )
        incoming = [incoming.astype(BF16).reshape(tile_blocks, half, width)]
    features, *sends = pl.pallas_call(
        functools.partial(merge_kernel, swaps),
        out_shape=(block_shape,) + (rim_shape,) * len(swaps),
        in_specs=[SMEM] + [VMEM] * len(incoming),
        out_specs=(VMEM,) * (1 + len(swaps)),
        compiler_params=PARAMS,
    )(halo, *incoming)
    received = swap_all(swaps, sends)

    pairs_total = padded * pair_slots
    own_columns = pl.pallas_call(
        functools.partial(own_columns_kernel, chunk),
        out_shape=shape((half, pairs_total), BF16),
        in_specs=[VMEM] * 2,
        out_specs=VMEM,
        compiler_params=PARAMS,
    )(features, source_rows)
    part, columns = pl.pallas_call(
        functools.partial(forward_kernel, tile_blocks // 2, chunk),
        out_shape=(shape((channels, own_total), F32), shape((half, pairs_total), BF16)),
        in_specs=[VMEM] * (4 + len(swaps)),
        out_specs=(VMEM, VMEM),
        scratch_shapes=[
            pltpu.VMEM((2 * channels, pairs_total), BF16),
            pltpu.VMEM((span, pairs_total), BF16),
        ],
        compiler_params=PARAMS,
    )(own_columns, source_rows, target_rows, w_rows_t, *received)
    other = lax.ppermute(part, "chan", [(0, 1), (1, 0)])

    portions = depths if merged else 1
    portion = (padded // portions * half, channels)
    activations, grad_columns, keep, *cross = pl.pallas_call(
        functools.partial(weight_grad_kernel, chunk // 2),
        out_shape=(block_shape, shape((channels, pairs_total), BF16), shape(portion, F32))
        + (shape(portion, BF16),) * (portions - 1),
        in_specs=[VMEM] * 5,
        out_specs=(VMEM,) * (2 + portions),
        scratch_shapes=[pltpu.VMEM((portions, *portion), F32)],
        compiler_params=PARAMS,
    )(part, other, cotangent_full, target_rows, columns)
    scale = float(tile_count * pair_slots) ** (-0.5)
    own_grad, *rims = pl.pallas_call(
        input_grad_kernel,
        out_shape=(shape((tile_blocks, half, width), F32),) + (rim_shape,) * len(swaps),
        in_specs=[VMEM] * 3,
        out_specs=(VMEM,) * (1 + len(swaps)),
        scratch_shapes=[
            pltpu.VMEM((held_total // 2 * half, pairs_total), BF16),
            pltpu.VMEM((span, pairs_total), BF16),
        ],
        compiler_params=PARAMS,
    )(grad_columns, source_rows, w_rows)
    returned = swap_all(swaps, rims)
    if merged:
        rows = portion[0] // tile_rows
        own_rows = tile_blocks * half
        column_rows = tile_rows * own_rows
        grad, share, *sends = pl.pallas_call(
            functools.partial(collect_kernel, swaps),
            out_shape=(shape((own_rows, width), BF16), shape((rows, channels), F32))
            + (shape((own_rows + rows, width), BF16),) * (tile_rows - 1),
            in_specs=[SMEM] + [VMEM] * (3 + len(swaps)),
            out_specs=(VMEM,) * (1 + tile_rows),
            scratch_shapes=[
                pltpu.VMEM((tile_blocks, half, width), F32),
                pltpu.VMEM(portion, F32),
            ],
            compiler_params=PARAMS,
        )(halo, own_grad, keep, across(cross[0]), *returned)
        received = to_rows([share, *sends], tile_rows)
        early = [across(grad), across(received[1])]
        received, early = lax.optimization_barrier((received, early))
        bulk, shard = pl.pallas_call(
            functools.partial(column_kernel, 1),
            out_shape=(
                shape((column_rows - 2 * own_rows + rows, channels), BF16),
                shape((rows, channels), BF16),
            ),
            in_specs=[VMEM] * tile_rows,
            out_specs=(VMEM,) * 2,
            compiler_params=PARAMS,
        )(*received)
        other_bulk = across(bulk)
        shards = to_rows([shard] * tile_rows, tile_rows)
        grad_log = pl.pallas_call(
            spread_kernel,
            out_shape=shape((log_count, half, width), BF16),
            in_specs=[SMEM] + [VMEM] * 6,
            out_specs=VMEM,
            scratch_shapes=[pltpu.VMEM((2 * column_rows, width), BF16)],
            compiler_params=PARAMS,
        )(place, grad, received[1], bulk, *early, other_bulk)
        far_shards = [across(part) for part in shards[1:]]
        far_shards, grad_log = lax.optimization_barrier((far_shards, grad_log))
        grad_weight = pl.pallas_call(
            functools.partial(weight_kernel, scale, tile_rows),
            out_shape=shape((offsets * half, channels), F32),
            in_specs=[VMEM] * (2 * tile_rows),
            out_specs=VMEM,
            scratch_shapes=[pltpu.VMEM((padded * half, channels), F32)],
            compiler_params=PARAMS,
        )(*shards, other_bulk, *far_shards)
    else:
        tile_grad = pl.pallas_call(
            functools.partial(tile_grad_kernel, swaps),
            out_shape=block_shape,
            in_specs=[SMEM] + [VMEM] * (1 + len(swaps)),
            out_specs=VMEM,
            scratch_shapes=[pltpu.VMEM((tile_blocks, half, width), F32)],
            compiler_params=PARAMS,
        )(halo, own_grad, *returned)
        back_blocks = jnp.dot(
            place_table.T,
            tile_grad.reshape(tile_blocks, half * width),
            preferred_element_type=F32,
        ).astype(BF16)
        back = relay(back_blocks.reshape(tile_count, capacity, half, width))
        grad_log = jnp.dot(
            pick_table.T,
            back.reshape(tile_count * capacity, half * width),
            preferred_element_type=F32,
        ).astype(BF16)
        grad_weight = lax.psum(keep[: offsets * half], TILES_AXES) * scale
    return (
        activations[None],
        grad_log.reshape(1, log_count, half, width),
        grad_weight.reshape(offsets, half, channels),
    )


def solution(mesh):
    split = ("groups", "tile", "depth")
    in_specs = (
        P(split, None, "chan", None),
        P(split, None, None),
        P(split, None, None),
        P(split, None, None),
        P(split, None, None),
        P(split, None, None),
        P(split, None),
        P(),
        P(split, None, "chan", None),
    )
    out_specs = (
        P(split, None, "chan", None),
        P(split, None, "chan", None),
        P("groups", "chan", None),
    )
    return jax.shard_map(local, mesh=mesh, in_specs=in_specs, out_specs=out_specs, check_vma=False)
```

```python
import functools

import jax
import jax.numpy as jnp
from jax import lax
from jax.experimental import pallas as pl
from jax.experimental.pallas import tpu as pltpu
from jax.sharding import PartitionSpec as P

F32 = jnp.float32
BF16 = jnp.bfloat16
TILES_AXES = ("tile", "depth")
VMEM = pl.BlockSpec(memory_space=pltpu.VMEM)
SMEM = pl.BlockSpec(memory_space=pltpu.SMEM)
PARAMS = pltpu.CompilerParams(vmem_limit_bytes=24 * 1024 * 1024)


def shape(dims, dtype):
    return jax.ShapeDtypeStruct(dims, dtype)


def pair_lists(size):
    return [
        [pair for i in range(first, size - 1, 2) for pair in ((i, i + 1), (i + 1, i))]
        for first in (0, 1)
    ]


def exchanges(tile_rows, depths):
    found = []
    for axis, size in (("tile", tile_rows), ("depth", depths)):
        for parity, pairs in enumerate(pair_lists(size)):
            if pairs:
                found.append((axis, parity, pairs))
    return found


def direction(axis, parity):
    place = lax.axis_index(axis) % 2
    upper = (place == parity).astype(jnp.int32)
    return upper + (0 if axis == "tile" else 2)


def xor_pairs(size, distance):
    return [(i, i ^ distance) for i in range(size)]


def merge_column(jx, rows_away, depths, tile_blocks, send_ref, tables, log_ref, emit):
    i, j = lax.axis_index("tile"), lax.axis_index("depth")
    me = i * depths + j
    half, width = log_ref.shape[1:]
    for d in rows_away:
        p = (i ^ d) * depths + (j ^ jx)
        totals = [jnp.zeros((half, width), F32) for _ in range(tile_blocks)]
        for c in range(send_ref.shape[1]):
            block = send_ref[p, c]
            wanted = jnp.where(block >= 0, tables(d, me, c), -1)
            rows = log_ref[jnp.maximum(block, 0)].astype(F32)
            for m in range(tile_blocks):
                totals[m] = totals[m] + rows * jnp.where(wanted == m, 1.0, 0.0)
        for m in range(tile_blocks):
            emit(d, m, totals[m])


def copy_kernel(in_ref, out_ref):
    out_ref[...] = in_ref[...]


def far_kernel(rows_away, depths, tile_blocks, send_ref, far_ref, log_ref, out_ref):
    def emit(d, m, total):
        out_ref[(d - rows_away[0]) * tile_blocks + m] = total.astype(BF16)

    merge_column(
        1, rows_away, depths, tile_blocks, send_ref, lambda *at: far_ref[at], log_ref, emit
    )


def near_kernel(tile_rows, depths, tile_blocks, *refs):
    send_ref, tables, log_ref, outs = refs[0], refs[1:-3], refs[-3], refs[-2:]
    per = tile_rows // len(outs)

    def emit(d, m, total):
        outs[d // per][(d % per) * tile_blocks + m] = total

    merge_column(
        0,
        range(tile_rows),
        depths,
        tile_blocks,
        send_ref,
        lambda d, *at: tables[d][at],
        log_ref,
        emit,
    )


def place_kernel(tile_rows, depths, tile_blocks, *refs):
    send_ref, tables, far_ref, place_ref = refs[0], refs[1:-2], refs[-2], refs[-1]
    i, j = lax.axis_index("tile"), lax.axis_index("depth")
    me = i * depths + j
    for jx in range(depths):
        for d in range(tile_rows):
            p = (i ^ d) * depths + (j ^ jx)
            for c in range(send_ref.shape[1]):
                block = send_ref[p, c]
                target = far_ref[d, me, c] if jx else tables[d][me, c]
                spot = jnp.where(block >= 0, block, place_ref.shape[0] - 1)
                place_ref[spot] = (jx * tile_rows + d) * tile_blocks + target


def add_kernel(near_ref, far_ref, *outs):
    count = near_ref.shape[0] // len(outs)
    for n, ref in enumerate(outs):
        for m in range(count):
            at = n * count + m
            ref[m] = (near_ref[at] + far_ref[at].astype(F32)).astype(ref.dtype)


def merge_kernel(swaps, halo_ref, *refs):
    incoming, features_ref = refs[: -1 - len(swaps)], refs[-1 - len(swaps)]
    sends = refs[-len(swaps) :] if swaps else ()
    for m in range(features_ref.shape[0]):
        total = incoming[0][m].astype(F32)
        for ref in incoming[1:]:
            total = total + ref[m].astype(F32)
        features_ref[m] = total.astype(BF16)
    pick_blocks(swaps, features_ref, halo_ref, sends)


def pick_blocks(swaps, features_ref, halo_ref, sends):
    for (axis, parity, _), send_ref in zip(swaps, sends):
        group = direction(axis, parity)
        for b in range(send_ref.shape[0]):
            send_ref[b] = features_ref[halo_ref[group, b]]


def table_row(ref, k):
    return ref[k : k + 1, :]


def one_hot(low, height):
    rows = lax.broadcasted_iota(jnp.int32, (height, low.shape[1]), 0).astype(F32).astype(BF16)
    low = low.astype(F32).astype(BF16)
    return jnp.where(rows == low, jnp.ones((), BF16), jnp.zeros((), BF16))


def pick_fold(fold, parts):
    picked = jnp.zeros_like(parts[0])
    for f, part in enumerate(parts):
        picked = jnp.where(fold == f, part, picked)
    return picked


def mask_fold(fold, f, part):
    return jnp.where(fold == f, part, jnp.zeros_like(part))


def gather_folds(folded, rows_ref, first_fold, chunk, half, base_of, emit):
    offsets, width = rows_ref.shape
    span = 2 * width
    for first in range(0, offsets, chunk):
        rows = [table_row(rows_ref, k) for k in range(first, first + chunk)]
        table = jnp.concatenate([one_hot(r & (span - 1), span) for r in rows], 1)
        gathered = jnp.dot(folded, table, preferred_element_type=F32).astype(BF16)
        for n, row in enumerate(rows):
            fold = (row // span).astype(F32).astype(BF16)
            picked = base_of(first + n)
            for f in range(folded.shape[0] // half):
                part = gathered[f * half : (f + 1) * half, n * width : (n + 1) * width]
                picked = jnp.where(fold == first_fold + f, part, picked)
            emit(first + n, picked)


def fold_blocks(blocks):
    return jnp.concatenate(
        [jnp.concatenate(blocks[n : n + 2], 1) for n in range(0, len(blocks), 2)], 0
    )


def own_columns_kernel(chunk, features_ref, source_ref, out_ref):
    count, half, width = features_ref.shape
    zero = jnp.zeros((half, width), BF16)

    def emit(k, picked):
        out_ref[:, k * width : (k + 1) * width] = picked

    folded = fold_blocks([features_ref[b] for b in range(count)])
    gather_folds(folded, source_ref, 0, chunk, half, lambda k: zero, emit)


def forward_kernel(own_folds, chunk, *refs):
    own_ref, source_ref, target_ref, weight_ref = refs[:4]
    received, (part_ref, columns_ref, values, places) = refs[4:-4], refs[-4:]
    channels, half = weight_ref.shape[1:]
    offsets, width = source_ref.shape
    span = 2 * width

    def lanes(k):
        return slice(k * width, (k + 1) * width)

    def emit(k, picked):
        columns_ref[:, lanes(k)] = picked

    def multiply(k):
        product = jnp.dot(weight_ref[k], columns_ref[:, lanes(k)], preferred_element_type=F32)
        product = product.astype(BF16)
        target = table_row(target_ref, k)
        fold = (target // span).astype(F32).astype(BF16)
        places[:, lanes(k)] = one_hot(target & (span - 1), span)
        for f in range(2):
            values[f * channels : (f + 1) * channels, lanes(k)] = mask_fold(fold, f, product)

    blocks = [ref[b] for ref in received for b in range(ref.shape[0])]
    if blocks:
        gather_folds(
            fold_blocks(blocks),
            source_ref,
            own_folds,
            chunk,
            half,
            lambda k: own_ref[:, lanes(k)],
            emit,
        )
    else:
        for k in range(offsets):
            emit(k, own_ref[:, lanes(k)])
    for k in range(offsets):
        multiply(k)
    total = lax.dot_general(
        values[...], places[...], (((1,), (1,)), ((), ())), preferred_element_type=F32
    )
    part_ref[:, :span] = total[:channels]
    part_ref[:, span:] = total[channels:]


def weight_grad_kernel(chunk, *refs):
    part_ref, other_ref, cotangent_ref, target_ref, columns_ref = refs[:5]
    act_ref, grad_columns_ref = refs[5:7]
    portions, held = refs[7:-1], refs[-1]
    tile_blocks, channels, width = cotangent_ref.shape
    half = columns_ref.shape[0]
    offsets = target_ref.shape[0]
    span = 2 * width
    portion = offsets // len(portions)
    here = lax.axis_index("depth") if len(portions) > 1 else 0
    preact = part_ref[...] + other_ref[...]
    gate = 1.0 / (1.0 + jnp.exp(-preact))
    cotangent = jnp.concatenate([cotangent_ref[b] for b in range(tile_blocks)], 1).astype(F32)
    grad = (cotangent * gate * (1.0 + preact * (1.0 - gate))).astype(BF16)
    folded = jnp.concatenate([grad[:, :span], grad[:, span:]], 0)
    for first in range(0, offsets, chunk):
        ks = range(first, first + chunk)
        rows = [table_row(target_ref, k) for k in ks]
        table = jnp.concatenate([one_hot(r & (span - 1), span) for r in rows], 1)
        gathered = jnp.dot(folded, table, preferred_element_type=F32).astype(BF16)
        for n, k in enumerate(ks):
            inside = slice(n * width, (n + 1) * width)
            lanes = slice(k * width, (k + 1) * width)
            fold = (rows[n] // span).astype(F32).astype(BF16)
            picked = pick_fold(fold, [gathered[:channels, inside], gathered[channels:, inside]])
            grad_columns_ref[:, lanes] = picked
    for k in range(offsets):
        lanes = slice(k * width, (k + 1) * width)
        row = (k % portion) * half
        held[(k // portion) ^ here, row : row + half, :] = lax.dot_general(
            columns_ref[:, lanes],
            grad_columns_ref[:, lanes],
            (((1,), (1,)), ((), ())),
            preferred_element_type=F32,
        )
    for n, ref in enumerate(portions):
        ref[...] = held[n].astype(ref.dtype)
    start = pl.multiple_of(lax.axis_index("chan") * half, half)
    own = part_ref[pl.ds(start, half), :] + other_ref[pl.ds(start, half), :]
    own = own / (1.0 + jnp.exp(-own))
    for b in range(tile_blocks):
        act_ref[b] = own[:, b * width : (b + 1) * width].astype(BF16)


def input_grad_kernel(grad_columns_ref, source_ref, weight_ref, own_ref, *refs):
    rims, (values, places) = refs[:-2], refs[-2:]
    tile_blocks = own_ref.shape[0]
    offsets, half, _ = weight_ref.shape
    width = source_ref.shape[1]
    span = 2 * width
    folds = values.shape[0] // half
    for k in range(offsets):
        lanes = slice(k * width, (k + 1) * width)
        returned = jnp.dot(
            weight_ref[k], grad_columns_ref[:, lanes], preferred_element_type=F32
        ).astype(BF16)
        source = table_row(source_ref, k)
        fold = (source // span).astype(F32).astype(BF16)
        places[:, lanes] = one_hot(source & (span - 1), span)
        for f in range(folds):
            values[f * half : (f + 1) * half, lanes] = mask_fold(fold, f, returned)
    total = lax.dot_general(
        values[...], places[...], (((1,), (1,)), ((), ())), preferred_element_type=F32
    )

    def block(b):
        return total[(b // 2) * half : (b // 2 + 1) * half, (b % 2) * width : (b % 2 + 1) * width]

    for b in range(tile_blocks):
        own_ref[b] = block(b)
    place = tile_blocks
    for rim in rims:
        for b in range(rim.shape[0]):
            rim[b] = block(place).astype(BF16)
            place += 1


def add_rims(swaps, halo_ref, total, received):
    for (axis, parity, _), ref in zip(swaps, received):
        group = direction(axis, parity)
        for b in range(ref.shape[0]):
            where = halo_ref[group, b]
            total[where] = total[where] + ref[b].astype(F32)


def tile_grad_kernel(swaps, halo_ref, own_ref, *refs):
    received, (out_ref, total) = refs[:-2], refs[-2:]
    total[...] = own_ref[...]
    add_rims(swaps, halo_ref, total, received)
    out_ref[...] = total[...].astype(BF16)


def collect_kernel(swaps, halo_ref, own_ref, keep_ref, crossed_ref, *refs):
    received, refs = refs[: len(swaps)], refs[len(swaps) :]
    (grad_ref, share_ref, *sends), (total, terms) = refs[:-2], refs[-2:]
    blocks, half, _ = own_ref.shape
    terms[...] = keep_ref[...] + crossed_ref[...].astype(F32)
    total[...] = own_ref[...]
    add_rims(swaps, halo_ref, total, received)
    for b in range(blocks):
        grad_ref[b * half : (b + 1) * half, :] = total[b].astype(BF16)
    i = lax.axis_index("tile")
    rows = share_ref.shape[0]
    for d, ref in enumerate((share_ref, *sends)):
        share = terms[pl.ds(pl.multiple_of((i ^ d) * rows, rows), rows), :]
        if d:
            ref[: blocks * half, :] = grad_ref[...]
            ref[blocks * half :, :] = share.astype(BF16)
        else:
            ref[...] = share


def column_kernel(early, share_ref, *refs):
    received, (bulk_ref, shard_ref) = refs[:-2], refs[-2:]
    rows = received[0].shape[0] - share_ref.shape[0]
    total = share_ref[...]
    for d, ref in enumerate(received):
        total = total + ref[rows:, :].astype(F32)
        if d >= early:
            bulk_ref[(d - early) * rows : (d - early + 1) * rows, :] = ref[:rows, :]
    shard_ref[...] = total.astype(BF16)
    bulk_ref[(len(received) - early) * rows :, :] = shard_ref[...]


def spread_kernel(place_ref, *refs):
    parts, (out_ref, held) = refs[:-2], refs[-2:]
    height = out_ref.shape[1]
    rows = parts[0].shape[0]
    first = 0
    for n, ref in enumerate(parts):
        count = rows if n % 3 < 2 else held.shape[0] // 2 - 2 * rows
        held[first : first + count, :] = ref[:count, :]
        first += count
    for b in range(out_ref.shape[0]):
        start = pl.multiple_of(place_ref[b] * height, height)
        out_ref[b] = held[pl.ds(start, height), :]


def weight_kernel(scale, tile_rows, *refs):
    near, (bulk_ref, *far), (out_ref, held) = refs[:tile_rows], refs[tile_rows:-2], refs[-2:]
    i, j = lax.axis_index("tile"), lax.axis_index("depth")
    rows = near[0].shape[0]
    for jx in range(2):
        for d in range(tile_rows):
            if jx == 0:
                shard = near[d][...]
            elif d == 0:
                shard = bulk_ref[bulk_ref.shape[0] - rows :, :]
            else:
                shard = far[d - 1][...]
            start = pl.multiple_of(((j ^ jx) * tile_rows + (i ^ d)) * rows, rows)
            held[pl.ds(start, rows), :] = shard
    out_ref[...] = held[: out_ref.shape[0], :].astype(F32) * scale


def swap_all(swaps, arrays):
    return [
        lax.ppermute(array, axis, pairs) for (axis, _, pairs), array in zip(swaps, arrays)
    ]


def to_rows(arrays, tile_rows):
    return [arrays[0]] + [
        lax.ppermute(arrays[d], "tile", xor_pairs(tile_rows, d)) for d in range(1, tile_rows)
    ]


def across(array):
    return lax.ppermute(array, "depth", [(0, 1), (1, 0)])


def relay(outgoing):
    return lax.all_to_all(outgoing, TILES_AXES, split_axis=0, concat_axis=0, tiled=True)


def local(
    log_features, send_slot, merge_slot, halo_list, in_rows, out_rows, pair_count, weight, cotangent
):
    tile_rows = lax.axis_size("tile")
    depths = lax.axis_size("depth")
    tile_count = tile_rows * depths
    log_blocks = log_features[0]
    log_count, half, width = log_blocks.shape
    tile_blocks = cotangent.shape[1]
    offsets, channels, _ = weight.shape
    capacity = send_slot.shape[2]
    rim_count = halo_list.shape[2]
    pair_slots = in_rows.shape[2]
    own_total = tile_blocks * width
    span = 2 * width
    chunk = 28
    padded = -(-offsets // chunk) * chunk
    swaps = exchanges(tile_rows, depths)
    merged = (tile_rows, depths) == (4, 2) and capacity >= tile_blocks
    send, merge, halo = send_slot[0], merge_slot[0], halo_list[0]

    block_of = in_rows[0] // width
    group_of = (block_of - tile_blocks) // rim_count
    held_total = tile_blocks + len(swaps) * rim_count
    new_block = jnp.where(block_of < tile_blocks, block_of, held_total)
    for place, (axis, parity, _) in enumerate(swaps):
        hit = (block_of >= tile_blocks) & (group_of == direction(axis, parity))
        inside = (block_of - tile_blocks) % rim_count
        new_block = jnp.where(hit, tile_blocks + place * rim_count + inside, new_block)
    live = jnp.arange(pair_slots, dtype=jnp.int32)[None, :] < pair_count[0][:, None]
    source_rows = jnp.where(live, new_block * width + in_rows[0] % width, held_total * width)
    target_rows = jnp.where(live, out_rows[0], own_total)
    extra = ((0, padded - offsets), (0, 0))
    source_rows = jnp.pad(source_rows, extra, constant_values=held_total * width)
    target_rows = jnp.pad(target_rows, extra, constant_values=own_total)
    w_rows = lax.dynamic_slice_in_dim(weight, lax.axis_index("chan") * half, half, 1)
    w_rows = jnp.pad(w_rows, ((0, padded - offsets), (0, 0), (0, 0)))
    w_rows_t = w_rows.transpose(0, 2, 1)
    cotangent_full = lax.all_gather(cotangent[0], "chan", axis=1, tiled=True)

    rim_shape = shape((rim_count, half, width), BF16)
    block_shape = shape((tile_blocks, half, width), BF16)
    if merged:
        near = to_rows([merge] * tile_rows, tile_rows)
        log_blocks = pl.pallas_call(
            copy_kernel,
            out_shape=shape(log_blocks.shape, BF16),
            in_specs=[VMEM],
            out_specs=VMEM,
            compiler_params=PARAMS,
        )(log_blocks)
        stacked, log_blocks = lax.optimization_barrier((jnp.stack(near), log_blocks))
        far = across(stacked)
        held_blocks = (tile_rows // 2 * tile_blocks, half, width)
        def far_sums(rows_away):
            return across(
                pl.pallas_call(
                    functools.partial(far_kernel, rows_away, depths, tile_blocks),
                    out_shape=shape(held_blocks, BF16),
                    in_specs=[SMEM] * 2 + [VMEM],
                    out_specs=VMEM,
                    compiler_params=PARAMS,
                )(send, far, log_blocks)
            )

        far_high = far_sums(range(tile_rows // 2, tile_rows))
        far_low = far_sums(range(tile_rows // 2))
        near_low, near_high = pl.pallas_call(
            functools.partial(near_kernel, tile_rows, depths, tile_blocks),
            out_shape=(shape(held_blocks, F32),) * 2,
            in_specs=[SMEM] * (1 + tile_rows) + [VMEM],
            out_specs=(VMEM,) * 2,
            compiler_params=PARAMS,
        )(send, *near, log_blocks)
        place = pl.pallas_call(
            functools.partial(place_kernel, tile_rows, depths, tile_blocks),
            out_shape=shape((log_count + 1,), jnp.int32),
            in_specs=[SMEM] * (2 + tile_rows),
            out_specs=SMEM,
            compiler_params=PARAMS,
        )(send, *near, far)
        add = functools.partial(
            pl.pallas_call,
            add_kernel,
            in_specs=[VMEM] * 2,
            out_specs=(VMEM,) * 2,
            compiler_params=PARAMS,
        )
        high = add(out_shape=(block_shape,) * 2)(near_high, far_high)
        low = add(out_shape=(shape((tile_blocks, half, width), F32), block_shape))(
            near_low, far_low
        )
        incoming = to_rows([*low, *high], tile_rows)
        incoming, place = lax.optimization_barrier((incoming, place))
    else:
        pick_table = (
            send.reshape(-1)[:, None] == jnp.arange(log_count, dtype=jnp.int32)[None, :]
        ).astype(BF16)
        outgoing = jnp.dot(
            pick_table, log_blocks.reshape(log_count, half * width), preferred_element_type=F32
        ).astype(BF16)
        incoming = relay(outgoing.reshape(tile_count, capacity, half, width))
        place_table = (
            jnp.arange(tile_blocks, dtype=jnp.int32)[:, None] == merge.reshape(-1)[None, :]
        ).astype(BF16)
        incoming = jnp.dot(
            place_table,
            incoming.reshape(tile_count * capacity, half * width),
            preferred_element_type=F32,
        )
        incoming = [incoming.astype(BF16).reshape(tile_blocks, half, width)]
    features, *sends = pl.pallas_call(
        functools.partial(merge_kernel, swaps),
        out_shape=(block_shape,) + (rim_shape,) * len(swaps),
        in_specs=[SMEM] + [VMEM] * len(incoming),
        out_specs=(VMEM,) * (1 + len(swaps)),
        compiler_params=PARAMS,
    )(halo, *incoming)
    received = swap_all(swaps, sends)

    pairs_total = padded * pair_slots
    own_columns = pl.pallas_call(
        functools.partial(own_columns_kernel, chunk),
        out_shape=shape((half, pairs_total), BF16),
        in_specs=[VMEM] * 2,
        out_specs=VMEM,
        compiler_params=PARAMS,
    )(features, source_rows)
    part, columns = pl.pallas_call(
        functools.partial(forward_kernel, tile_blocks // 2, chunk),
        out_shape=(shape((channels, own_total), F32), shape((half, pairs_total), BF16)),
        in_specs=[VMEM] * (4 + len(swaps)),
        out_specs=(VMEM, VMEM),
        scratch_shapes=[
            pltpu.VMEM((2 * channels, pairs_total), BF16),
            pltpu.VMEM((span, pairs_total), BF16),
        ],
        compiler_params=PARAMS,
    )(own_columns, source_rows, target_rows, w_rows_t, *received)
    other = lax.ppermute(part, "chan", [(0, 1), (1, 0)])

    portions = depths if merged else 1
    portion = (padded // portions * half, channels)
    activations, grad_columns, keep, *cross = pl.pallas_call(
        functools.partial(weight_grad_kernel, chunk // 2),
        out_shape=(block_shape, shape((channels, pairs_total), BF16), shape(portion, F32))
        + (shape(portion, BF16),) * (portions - 1),
        in_specs=[VMEM] * 5,
        out_specs=(VMEM,) * (2 + portions),
        scratch_shapes=[pltpu.VMEM((portions, *portion), F32)],
        compiler_params=PARAMS,
    )(part, other, cotangent_full, target_rows, columns)
    scale = float(tile_count * pair_slots) ** (-0.5)
    own_grad, *rims = pl.pallas_call(
        input_grad_kernel,
        out_shape=(shape((tile_blocks, half, width), F32),) + (rim_shape,) * len(swaps),
        in_specs=[VMEM] * 3,
        out_specs=(VMEM,) * (1 + len(swaps)),
        scratch_shapes=[
            pltpu.VMEM((held_total // 2 * half, pairs_total), BF16),
            pltpu.VMEM((span, pairs_total), BF16),
        ],
        compiler_params=PARAMS,
    )(grad_columns, source_rows, w_rows)
    returned = swap_all(swaps, rims)
    if merged:
        rows = portion[0] // tile_rows
        own_rows = tile_blocks * half
        column_rows = tile_rows * own_rows
        grad, share, *sends = pl.pallas_call(
            functools.partial(collect_kernel, swaps),
            out_shape=(shape((own_rows, width), BF16), shape((rows, channels), F32))
            + (shape((own_rows + rows, width), BF16),) * (tile_rows - 1),
            in_specs=[SMEM] + [VMEM] * (3 + len(swaps)),
            out_specs=(VMEM,) * (1 + tile_rows),
            scratch_shapes=[
                pltpu.VMEM((tile_blocks, half, width), F32),
                pltpu.VMEM(portion, F32),
            ],
            compiler_params=PARAMS,
        )(halo, own_grad, keep, across(cross[0]), *returned)
        received = to_rows([share, *sends], tile_rows)
        early = [across(grad), across(received[1])]
        received, early = lax.optimization_barrier((received, early))
        bulk, shard = pl.pallas_call(
            functools.partial(column_kernel, 1),
            out_shape=(
                shape((column_rows - 2 * own_rows + rows, channels), BF16),
                shape((rows, channels), BF16),
            ),
            in_specs=[VMEM] * tile_rows,
            out_specs=(VMEM,) * 2,
            compiler_params=PARAMS,
        )(*received)
        other_bulk = across(bulk)
        shards = to_rows([shard] * tile_rows, tile_rows)
        grad_log = pl.pallas_call(
            spread_kernel,
            out_shape=shape((log_count, half, width), BF16),
            in_specs=[SMEM] + [VMEM] * 6,
            out_specs=VMEM,
            scratch_shapes=[pltpu.VMEM((2 * column_rows, width), BF16)],
            compiler_params=PARAMS,
        )(place, grad, received[1], bulk, *early, other_bulk)
        far_shards = [across(part) for part in shards[1:]]
        far_shards, grad_log = lax.optimization_barrier((far_shards, grad_log))
        grad_weight = pl.pallas_call(
            functools.partial(weight_kernel, scale, tile_rows),
            out_shape=shape((offsets * half, channels), F32),
            in_specs=[VMEM] * (2 * tile_rows),
            out_specs=VMEM,
            scratch_shapes=[pltpu.VMEM((padded * half, channels), BF16)],
            compiler_params=PARAMS,
        )(*shards, other_bulk, *far_shards)
    else:
        tile_grad = pl.pallas_call(
            functools.partial(tile_grad_kernel, swaps),
            out_shape=block_shape,
            in_specs=[SMEM] + [VMEM] * (1 + len(swaps)),
            out_specs=VMEM,
            scratch_shapes=[pltpu.VMEM((tile_blocks, half, width), F32)],
            compiler_params=PARAMS,
        )(halo, own_grad, *returned)
        back_blocks = jnp.dot(
            place_table.T,
            tile_grad.reshape(tile_blocks, half * width),
            preferred_element_type=F32,
        ).astype(BF16)
        back = relay(back_blocks.reshape(tile_count, capacity, half, width))
        grad_log = jnp.dot(
            pick_table.T,
            back.reshape(tile_count * capacity, half * width),
            preferred_element_type=F32,
        ).astype(BF16)
        grad_weight = lax.psum(keep[: offsets * half], TILES_AXES) * scale
    return (
        activations[None],
        grad_log.reshape(1, log_count, half, width),
        grad_weight.reshape(offsets, half, channels),
    )


def solution(mesh):
    split = ("groups", "tile", "depth")
    in_specs = (
        P(split, None, "chan", None),
        P(split, None, None),
        P(split, None, None),
        P(split, None, None),
        P(split, None, None),
        P(split, None, None),
        P(split, None),
        P(),
        P(split, None, "chan", None),
    )
    out_specs = (
        P(split, None, "chan", None),
        P(split, None, "chan", None),
        P("groups", "chan", None),
    )
    return jax.shard_map(local, mesh=mesh, in_specs=in_specs, out_specs=out_specs, check_vma=False)
```
